128 devices in a mesh: mpo: 8 (over x, core), bond: 16 (over z, y).
Axes of the slice: x: 4, y: 4, z: 4, core: 2. Of those that a mesh axis runs over, the one named last changes fastest.
Arguments:
- environment: bfloat16 [4096, 40, 4096], P(None, 'mpo', 'bond'), may hold values from -60 to 60
- site_tensor: bfloat16 [4096, 4, 4096], P('bond'), may hold values from -0.09375 to 0.09375
- mpo_tensor: bfloat16 [40, 40, 4, 4], replicated, may hold values from -0.5 to 0.5
- sketch_site: bfloat16 [4096, 128], replicated, may hold values from -6 to 6
- sketch_expand: bfloat16 [128, 40, 4096], P('mpo'), may hold values from -60 to 60
- row_sectors: int32 [2, 4096, 4], P(None, 'bond'), may hold values from 0 to 5, as said below
- column_sectors: int32 [2, 128], replicated, may hold values from 0 to 5, as said below
Outputs:
- basis: bfloat16 [4096, 4, 128], P('bond')
- extended: float32 [128, 40, 128], P('bond', 'mpo')
The draws below stay inside these ranges and needn't reach their ends.
Inputs may be any that keep to these rules, and one draw needn't show every extreme that they name: `row_sectors`: every joined row's label pair is (4, 0) or (5, 1); the rows labelled (5, 1) are one run of 64 consecutive joined rows (a, s) in the order a then s. `column_sectors`: every column's label pair is (4, 0) or (5, 1); exactly 16 columns are labelled (5, 1).
All inputs are finite; a program needn't handle non-finite values.
Results may differ from the reference program's by a relative error of at most 0.0064.
Values may be sent and summed in bfloat16 or wider, within the bound.
No kernel may reach another device: no remote copies, remote signals or barrier semaphores. Data moves between devices by JAX's collectives and lax.ppermute only.
A program may use at most 128 MiB of HBM per device.

```python
import math
import jax
import jax.numpy as jnp
from jax import lax

CHI = 4096
W = 40
D = 4
K = 128


def draw_environment(key, part):
    base_key, scale_key = jax.random.split(jax.random.fold_in(key, 11))
    base = jnp.clip(jax.random.normal(base_key, (CHI, W, CHI), jnp.float32), -6.0, 6.0)
    scale = jnp.exp(jax.random.uniform(scale_key, (CHI, 1, 1), jnp.float32, 0.0, math.log(10.0)))
    return (base * scale).astype(jnp.bfloat16)


def draw_sketch_expand(key, part):
    base_key, scale_key = jax.random.split(jax.random.fold_in(key, 23))
    base = jnp.clip(jax.random.normal(base_key, (K, W, CHI), jnp.float32), -6.0, 6.0)
    scale = jnp.exp(jax.random.uniform(scale_key, (K, 1, 1), jnp.float32, 0.0, math.log(10.0)))
    return (base * scale).astype(jnp.bfloat16)


def draw_row_sectors(key, part):
    run_length = K // 2
    start = jax.random.randint(jax.random.fold_in(key, 31), (), 0, CHI * D - run_length + 1, dtype=jnp.int32)
    position = jnp.arange(CHI * D, dtype=jnp.int32)
    choose = ((position >= start) & (position < start + run_length)).astype(jnp.int32)
    return jnp.stack([4 + choose, choose]).reshape(2, CHI, D)


def draw_column_sectors(key, part):
    order = jax.random.permutation(jax.random.fold_in(key, 37), K)
    choose = (order < K // 8).astype(jnp.int32)
    return jnp.stack([4 + choose, choose])


def level_of(key, dims, shards, smallest, high):
    loudness, own = 1.0, jax.random.fold_in(key, 6)
    for dim, blocks in shards:
        draws = jnp.exp(jax.random.uniform(jax.random.fold_in(own, dim), (blocks,), jnp.float32, smallest / len(shards), high / len(shards)))
        loudness = loudness * jnp.repeat(draws, dims[dim] // blocks).reshape([-1 if axis == dim else 1 for axis in range(len(dims))])
    return loudness


def scatter_about(key, shape, deviation, limit, cuts=(), kind=jnp.bfloat16):
    values = deviation * jax.random.normal(key, shape, jnp.float32)
    if cuts:
        values = values * level_of(key, shape, cuts, -0.22, 0.18)
    return jnp.clip(values, -limit, limit).astype(kind)


def setup_inputs(seed: int = 0) -> dict:
    streams_of = jax.random.split(jax.random.key(seed), 8)
    environment = draw_environment(jax.random.fold_in(streams_of[7], 71), 0)
    site_tensor = scatter_about(streams_of[1], (CHI, D, CHI), CHI ** -0.5, 0.09375, ((0, 16),))
    mpo_tensor = scatter_about(streams_of[2], (W, W, D, D), (W * D) ** -0.5, 0.5)
    sketch_site = scatter_about(streams_of[3], (CHI, K), 1.0, 6.0)
    sketch_expand = draw_sketch_expand(jax.random.fold_in(streams_of[7], 71), 0)
    row_sectors = draw_row_sectors(jax.random.fold_in(streams_of[7], 71), 0)
    column_sectors = draw_column_sectors(jax.random.fold_in(streams_of[7], 71), 0)
    return dict(environment=environment, site_tensor=site_tensor, mpo_tensor=mpo_tensor, sketch_site=sketch_site, sketch_expand=sketch_expand, row_sectors=row_sectors, column_sectors=column_sectors)


mixing = 0.5
shift_tolerance = 1e-06

def sector_mask(row_labels, column_labels):
    match = (row_labels[0][:, :, None] == column_labels[0][None, None, :]) & (row_labels[1][:, :, None] == column_labels[1][None, None, :])
    return match.astype(jnp.float32)

def reference(environment, site_tensor, mpo_tensor, sketch_site, sketch_expand, row_sectors, column_sectors):
    highest_accuracy = lax.Precision.HIGHEST
    site_flat = site_tensor.reshape(CHI * D, CHI).astype(jnp.float32)
    indices = jnp.arange(W, dtype=jnp.int32)

    def sketch_one(index):
        random_probe_matrix = lax.dynamic_index_in_dim(sketch_expand, index, 1, keepdims=False).astype(jnp.float32)
        block = jnp.dot(site_flat, random_probe_matrix.T, precision=highest_accuracy)
        return jnp.transpose(block.reshape(CHI, D, K), (1, 2, 0)).astype(jnp.bfloat16)
    sketched = lax.map(sketch_one, indices)
    contracted = jnp.einsum('vwst,wtka->vska', mpo_tensor.astype(jnp.float32), sketched.astype(jnp.float32), precision=highest_accuracy).astype(jnp.bfloat16)

    def expand_one(index):
        env_w = lax.dynamic_index_in_dim(environment, index, 1, keepdims=False).astype(jnp.float32)
        part_w = lax.dynamic_index_in_dim(contracted, index, 0, keepdims=False).astype(jnp.float32).reshape(D * K, CHI)
        return jnp.dot(env_w, part_w.T, precision=highest_accuracy)
    enlarged_range = lax.optimization_barrier(jnp.sum(lax.map(expand_one, indices), axis=0)).reshape(CHI, D, K)
    site_y = jnp.dot(site_tensor.reshape(CHI * D, CHI).astype(jnp.float32), sketch_site.astype(jnp.float32), preferred_element_type=jnp.float32).reshape(CHI, D, K)
    mask = sector_mask(row_sectors, column_sectors)
    masked_site = site_y * mask
    filtered_enlarged = enlarged_range * mask
    mix = mixing * jnp.sqrt((jnp.sum(masked_site * masked_site) + shift_tolerance) / (jnp.sum(filtered_enlarged * filtered_enlarged) + shift_tolerance))
    combined = (masked_site + mix * filtered_enlarged).reshape(CHI * D, K)
    gram = jnp.dot(combined.T.astype(jnp.float32), combined.astype(jnp.float32), precision=highest_accuracy, preferred_element_type=jnp.float32)
    factor = jnp.linalg.cholesky(gram)
    solved = jax.scipy.linalg.solve_triangular(factor, combined.T, lower=True)
    basis = solved.T.reshape(CHI, D, K).astype(jnp.bfloat16)
    basis_flat = basis.reshape(CHI, D * K).astype(jnp.float32)

    def project_one(index):
        env_w = lax.dynamic_index_in_dim(environment, index, 1, keepdims=False).astype(jnp.float32)
        return jnp.dot(basis_flat.T, env_w, precision=highest_accuracy).astype(jnp.bfloat16)
    projected = lax.map(project_one, indices)

    def extend_one(index):
        proj_w = lax.dynamic_index_in_dim(projected, index, 0, keepdims=False).astype(jnp.float32)
        couple_merged = jnp.dot(proj_w, basis_flat, precision=highest_accuracy).reshape(D, K, D, K)
        hamiltonian_factor = lax.dynamic_index_in_dim(mpo_tensor, index, 0, keepdims=False).astype(jnp.float32)
        return jnp.einsum('uod,oydq->yuq', hamiltonian_factor, couple_merged, precision=highest_accuracy)
    extended = lax.optimization_barrier(jnp.sum(lax.map(extend_one, indices), axis=0))
    return (basis, extended)
```

```python
import jax
import jax.numpy as jnp
from jax import lax
from jax.sharding import Mesh
from jax.sharding import PartitionSpec as P

MPO = ("mpo_0", "mpo_1")
BOND = ("bond_0", "bond_1")
CHIPS = ("bond_0", "bond_1", "mpo_0")
CORE = "mpo_1"

mixing = 0.5
shift_tolerance = 1e-06
f32 = jnp.float32
bf16 = jnp.bfloat16


def sector_mask(row_labels, column_labels):
    match = (row_labels[0][:, :, None] == column_labels[0][None, None, :]) & (
        row_labels[1][:, :, None] == column_labels[1][None, None, :]
    )
    return match.astype(f32)


def summed_over_devices(parts):
    core = lax.axis_index(CORE)
    mine = lax.dynamic_index_in_dim(parts, core, 1, keepdims=False)
    other = lax.dynamic_index_in_dim(parts, 1 - core, 1, keepdims=False)
    got = lax.ppermute(other, CORE, [(0, 1), (1, 0)])
    half = (mine.astype(f32) + got.astype(f32)).astype(bf16)
    arrived = lax.all_to_all(half, CHIPS, 0, 0, tiled=True)
    return arrived.astype(f32).sum(axis=0)


def body(
    environment, site_tensor, mpo_tensor, sketch_site, sketch_expand, row_sectors, column_sectors
):
    mpo_index = lax.axis_index(MPO)
    chi, physical_width, _ = environment.shape
    local_rows, physical, _ = site_tensor.shape
    columns = column_sectors.shape[1]
    share = local_rows // 8
    chips = chi // (2 * share)
    mask_rows = sector_mask(row_sectors, column_sectors)

    site_y = jnp.einsum("asb,bk->ask", site_tensor, sketch_site, preferred_element_type=f32)
    site_local = (site_y * mask_rows).astype(bf16)
    site_all = lax.all_gather(site_local, BOND, axis=0, tiled=True)

    sketched = jnp.einsum(
        "asb,kwb->wska", site_tensor, sketch_expand, preferred_element_type=f32
    ).astype(bf16)
    applied = jnp.einsum(
        "vwst,wtka->vska", mpo_tensor, sketched, preferred_element_type=f32
    ).astype(bf16)
    contracted = lax.all_to_all(applied, MPO, split_axis=0, concat_axis=2, tiled=True)
    expand_part = jnp.einsum(
        "awc,wskc->ask", environment, contracted, preferred_element_type=f32
    ).astype(bf16)
    piece = summed_over_devices(
        expand_part.reshape(chips, 2, share, physical * columns)
    ).reshape(share, physical, columns)
    mask_share = lax.dynamic_slice_in_dim(mask_rows, mpo_index * share, share, 0)
    piece = (piece * mask_share).astype(bf16).reshape(share, physical * columns)
    half = lax.all_to_all(
        jnp.broadcast_to(piece[None], (chips, *piece.shape)), CHIPS, 0, 0, tiled=True
    )
    expand_all = lax.all_gather(half, CORE, axis=1).reshape(chi, physical, columns)

    def gram_of(left, right):
        return jnp.einsum("ask,asl->kl", left, right, preferred_element_type=f32)

    gram_site = gram_of(site_all, site_all)
    gram_cross = gram_of(site_all, expand_all)
    gram_expand = gram_of(expand_all, expand_all)
    mix = mixing * jnp.sqrt(
        (jnp.trace(gram_site) + shift_tolerance) / (jnp.trace(gram_expand) + shift_tolerance)
    )
    gram_total = gram_site + mix * (gram_cross + gram_cross.T) + mix * mix * gram_expand
    factor = jnp.linalg.cholesky(gram_total)
    inverse = jax.scipy.linalg.solve_triangular(factor, jnp.eye(columns, dtype=f32), lower=True)
    combined = site_all.astype(f32) + mix * expand_all.astype(f32)
    basis = jnp.einsum("ask,lk->asl", combined, inverse, precision=lax.Precision.HIGH).astype(bf16)
    bond_index = lax.axis_index(BOND)
    basis_local = lax.dynamic_slice_in_dim(basis, bond_index * local_rows, local_rows, 0)

    projected = jnp.einsum(
        "ax,awc->wxc", basis.reshape(chi, -1), environment, preferred_element_type=f32
    ).astype(bf16)
    paired = jnp.einsum(
        "wxc,cy->wxy",
        projected,
        basis_local.reshape(local_rows, -1),
        preferred_element_type=f32,
    ).reshape(physical_width, physical, columns, physical, columns)
    operator_rows = lax.dynamic_slice_in_dim(
        mpo_tensor, mpo_index * physical_width, physical_width, 0
    )
    share_out = jnp.einsum(
        "wvst,wsktl->kvl", operator_rows.astype(f32), paired, precision=lax.Precision.HIGH
    ).astype(bf16)
    kout, vout = columns // 16, mpo_tensor.shape[1] // 8
    parts = share_out.reshape(16, kout, 4, 2, vout, columns).transpose(0, 2, 3, 1, 4, 5)
    extended = summed_over_devices(parts.reshape(64, 2, kout, vout, columns))
    return (basis_local, extended)


def solution(mesh):
    torus = Mesh(mesh.devices.reshape(4, 2, 4, 4), ("mpo_0", "mpo_1", "bond_0", "bond_1"))
    placed = (
        P(None, MPO, BOND),
        P(BOND, None, None),
        P(),
        P(),
        P(MPO, None, None),
        P(None, BOND, None),
        P(),
    )
    return jax.shard_map(
        body,
        mesh=torus,
        in_specs=placed,
        out_specs=(P(BOND, None, None), P(BOND, MPO, None)),
        check_vma=False,
    )
```

```python
import jax
import jax.numpy as jnp
from jax import lax
from jax.experimental import pallas as pl
from jax.experimental.pallas import tpu as pltpu
from jax.sharding import Mesh
from jax.sharding import PartitionSpec as P

MPO = ("mpo_0", "mpo_1")
BOND = ("bond_0", "bond_1")
CHIPS = ("bond_0", "bond_1", "mpo_0")
CORE = "mpo_1"
SWAP = [(0, 1), (1, 0)]

mixing = 0.5
shift_tolerance = 1e-06
f32 = jnp.float32
bf16 = jnp.bfloat16
VMEM = 40 * 1024 * 1024


def sector_mask(row_labels, column_labels):
    match = (row_labels[0][:, :, None] == column_labels[0][None, None, :]) & (
        row_labels[1][:, :, None] == column_labels[1][None, None, :]
    )
    return match.astype(f32)


def dot(a, b, dims):
    return lax.dot_general(a, b, (dims, ((), ())), preferred_element_type=f32)


def cost(flops, size):
    return pl.CostEstimate(flops=flops, bytes_accessed=size, transcendentals=0)


def expand_half(core, env, contracted):
    width, blocks, _, share, depth = env.shape
    x = contracted.shape[1]
    k = share
    s = x // k
    step = 4

    def kernel(core_ref, e_ref, c_ref, o_ref):
        left = jnp.concatenate(
            [e_ref[w, :, 0].reshape(step * share, depth) for w in range(width)], axis=1
        )
        right = jnp.concatenate([c_ref[w] for w in range(width)], axis=1)
        total = dot(left, right, ((1,), (1,)))
        for i in range(s):
            o_ref[:, i] = total[:, i * k : (i + 1) * k].astype(bf16).reshape(step, share, k)

    return pl.pallas_call(
        kernel,
        grid_spec=pltpu.PrefetchScalarGridSpec(
            num_scalar_prefetch=1,
            grid=(blocks // step,),
            in_specs=[
                pl.BlockSpec((width, step, 1, share, depth), lambda i, core: (0, i, core[0], 0, 0)),
                pl.BlockSpec((width, x, depth), lambda i, core: (0, 0, 0)),
            ],
            out_specs=pl.BlockSpec((step, s, share, k), lambda i, core: (i, 0, 0, 0)),
        ),
        out_shape=jax.ShapeDtypeStruct((blocks, s, share, k), bf16),
        compiler_params=pltpu.CompilerParams(vmem_limit_bytes=VMEM),
        cost_estimate=cost(2 * width * blocks * share * depth * x, 9_000_000),
        name="expand_half",
    )(core, env, contracted)


def site_terms(env, site):
    width, blocks, rows, depth = env.shape
    s, k = site.shape[1:3]
    step = 2

    def kernel(e_ref, s_ref, x_ref, g_ref):
        first = pl.program_id(0) == 0
        left = jnp.concatenate([s_ref[z].reshape(s * k, rows) for z in range(step)], axis=1)

        def term(w):
            return dot(left, e_ref[w].reshape(step * rows, depth), ((1,), (0,)))

        wide = jnp.concatenate([left[i * k : (i + 1) * k] for i in range(s)], axis=1)
        gram = dot(wide, wide, ((1,), (1,)))

        @pl.when(first)
        def _():
            for w in range(width):
                x_ref[w] = term(w)
            g_ref[...] = gram

        @pl.when(jnp.logical_not(first))
        def _():
            for w in range(width):
                x_ref[w] += term(w)
            g_ref[...] += gram

    return pl.pallas_call(
        kernel,
        grid=(blocks // step,),
        in_specs=[
            pl.BlockSpec((width, step, rows, depth), lambda i: (0, i, 0, 0)),
            pl.BlockSpec((step, s, k, rows), lambda i: (i, 0, 0, 0)),
        ],
        out_specs=[
            pl.BlockSpec((width, s * k, depth), lambda i: (0, 0, 0)),
            pl.BlockSpec((k, k), lambda i: (0, 0)),
        ],
        out_shape=[
            jax.ShapeDtypeStruct((width, s * k, depth), f32),
            jax.ShapeDtypeStruct((k, k), f32),
        ],
        compiler_params=pltpu.CompilerParams(vmem_limit_bytes=VMEM),
        cost_estimate=cost(6_000_000_000, 17_000_000),
        name="site_terms",
    )(env, site)


def expand_step(e_ref, s_ref, h_ref):
    width, step, _, share, depth = e_ref.shape
    s, k = h_ref.shape[1:3]
    left = jnp.concatenate([h_ref[z].reshape(s * k, share) for z in range(step)], axis=1)
    terms = [
        lambda w=w: dot(left, e_ref[w, :, 0].reshape(step * share, depth), ((1,), (0,)))
        for w in range(width)
    ]
    wide = jnp.concatenate([left[i * k : (i + 1) * k] for i in range(s)], axis=1)
    site = jnp.concatenate([s_ref[z, i] for i in range(s) for z in range(step)], axis=1)
    gram = dot(wide, jnp.concatenate([wide, site], axis=0), ((1,), (1,)))
    return terms, gram


def expand_specs(width, step, share, depth, s, k):
    return [
        pl.BlockSpec((width, step, 1, share, depth), lambda i, sc: (0, i, sc[0], 0, 0)),
        pl.BlockSpec((step, s, k, share), lambda i, sc: (i, 0, 0, sc[0])),
        pl.BlockSpec((step, s, k, share), lambda i, sc: (i, 0, 0, 0)),
    ]


def expand_terms(core, env, site, half):
    width, blocks, _, share, depth = env.shape
    s, k = half.shape[1:3]
    step = 4

    def kernel(core_ref, e_ref, s_ref, h_ref, x_ref, g_ref):
        first = pl.program_id(0) == 0
        terms, gram = expand_step(e_ref, s_ref, h_ref)

        @pl.when(first)
        def _():
            for w in range(width):
                x_ref[w] = terms[w]()
            g_ref[...] = gram

        @pl.when(jnp.logical_not(first))
        def _():
            for w in range(width):
                x_ref[w] += terms[w]()
            g_ref[...] += gram

    return pl.pallas_call(
        kernel,
        grid_spec=pltpu.PrefetchScalarGridSpec(
            num_scalar_prefetch=1,
            grid=(blocks // step,),
            in_specs=expand_specs(width, step, share, depth, s, k),
            out_specs=[
                pl.BlockSpec((width, s * k, depth), lambda i, sc: (0, 0, 0)),
                pl.BlockSpec((k, 2 * k), lambda i, sc: (0, 0)),
            ],
        ),
        out_shape=[
            jax.ShapeDtypeStruct((width, s * k, depth), f32),
            jax.ShapeDtypeStruct((k, 2 * k), f32),
        ],
        compiler_params=pltpu.CompilerParams(vmem_limit_bytes=VMEM),
        cost_estimate=cost(3_300_000_000, 12_000_000),
        name="expand_terms",
    )(core, env, site, half)


def inverse_factor(a, nb):
    n = a.shape[0]
    count = n // 8
    rows = [a[8 * i : 8 * i + 8, :] for i in range(count)]
    lane = lax.broadcasted_iota(jnp.int32, (8, n), 1)
    sub = lax.broadcasted_iota(jnp.int32, (8, n), 0)

    def full(v):
        return jnp.broadcast_to(v, (8, n))

    for j in range(0, n, nb):
        b, o = j // 8, j % 8
        cols = {i: [full(rows[i][:, j + p : j + p + 1]) for p in range(nb)] for i in range(b, count)}
        lines = [full(rows[b][o + q : o + q + 1, :]) for q in range(nb)]
        pivots = [
            [full(cols[b][r][o + q : o + q + 1, :]) for r in range(q + 1)] for q in range(nb)
        ]
        scaled, ratio = [], {}
        for p in range(nb):
            inv = 1.0 / pivots[p][p]
            here = lane == j + p
            line = jnp.where(here, 1.0, lines[p]) * inv
            scaled.append(line)
            for q in range(p + 1, nb):
                ratio[q, p] = pivots[q][p] * inv
            for q in range(p + 1, nb):
                lines[q] = jnp.where(here, 0.0, lines[q]) - pivots[q][p] * line
                for r in range(p + 1, q + 1):
                    pivots[q][r] = pivots[q][r] - pivots[q][p] * ratio[r, p]
        for i in range(b, count):
            c = cols[i]
            value = rows[i]
            for p in range(nb):
                new = jnp.where(lane == j + p, 0.0, value) - c[p] * scaled[p]
                value = jnp.where(sub > o + p, new, value) if i == b else new
                for q in range(p + 1, nb):
                    c[q] = c[q] - c[p] * ratio[q, p]
            rows[i] = value
    w = jnp.concatenate(rows, axis=0)
    row = lax.broadcasted_iota(jnp.int32, (n, n), 0)
    col = lax.broadcasted_iota(jnp.int32, (n, n), 1)
    diagonal = jnp.sum(jnp.where(row == col, w, 0.0), axis=1, keepdims=True)
    unit = jnp.where(row > col, w, 0.0) + jnp.where(row == col, 1.0, 0.0)
    return unit * lax.rsqrt(diagonal)


def split(v):
    high = v.astype(bf16)
    return high, (v - high.astype(f32)).astype(bf16)


def finish(scalars, env, site, half, x_site, g_site, x_own, g_own, own, site_local):
    width, blocks, _, share, depth = env.shape
    s, k = half.shape[1:3]
    step = 4
    last = blocks // step - 1

    def kernel(
        sc_ref, e_ref, s_ref, h_ref, xs_ref, gs_ref, xo_ref, go_ref, own_ref, oth_ref, sl_ref,
        p_ref, b_ref, x_ref, g_ref,
    ):
        first = pl.program_id(0) == 0
        terms, gram = expand_step(e_ref, s_ref, h_ref)

        @pl.when(first)
        def _():
            for w in range(width):
                x_ref[w] = xo_ref[w] + terms[w]()
            g_ref[...] = go_ref[...] + gram

        @pl.when(jnp.logical_not(first))
        def _():
            for w in range(width):
                x_ref[w] += terms[w]()
            g_ref[...] += gram

        @pl.when(pl.program_id(0) == last)
        def _():
            gs = gs_ref[...]
            ge = g_ref[:, :k]
            gc = g_ref[:, k:]
            row = lax.broadcasted_iota(jnp.int32, (k, k), 0)
            col = lax.broadcasted_iota(jnp.int32, (k, k), 1)
            trace_site = jnp.sum(jnp.where(row == col, gs, 0.0), keepdims=True)
            trace_expand = jnp.sum(jnp.where(row == col, ge, 0.0), keepdims=True)
            mix = mixing * jnp.sqrt((trace_site + shift_tolerance) / (trace_expand + shift_tolerance))
            inverse = inverse_factor(gs + mix * (gc + gc.T) + (mix * mix) * ge, 8)
            high, low = split(inverse)
            both = jnp.concatenate([high, low], axis=1)

            def apply(v):
                vh, vl = split(v)
                return dot(both, jnp.concatenate([vh, vh], axis=0), ((1,), (0,))) + dot(
                    high, vl, ((1,), (0,))
                )

            for w in range(width):
                for i in range(s):
                    part = slice(i * k, (i + 1) * k)
                    p_ref[w, part] = apply(xs_ref[w, part] + mix * x_ref[w, part]).astype(bf16)
            even = sc_ref[0] == 1
            for i in range(s):
                a0 = own_ref[0, i].astype(f32)
                a1 = oth_ref[0, i].astype(f32)
                rows = jnp.concatenate(
                    [jnp.where(even, a0, a1), jnp.where(even, a1, a0)], axis=1
                )
                done = apply(sl_ref[i] + mix * rows)
                b_ref[:, i * k : (i + 1) * k] = done.T.astype(bf16)

    fixed3 = lambda i, sc: (0, 0, 0)
    fixed2 = lambda i, sc: (0, 0)
    return pl.pallas_call(
        kernel,
        grid_spec=pltpu.PrefetchScalarGridSpec(
            num_scalar_prefetch=1,
            grid=(blocks // step,),
            in_specs=expand_specs(width, step, share, depth, s, k)
            + [
                pl.BlockSpec((width, s * k, depth), fixed3),
                pl.BlockSpec((k, k), fixed2),
                pl.BlockSpec((width, s * k, depth), fixed3),
                pl.BlockSpec((k, 2 * k), fixed2),
                pl.BlockSpec((1, s, k, share), lambda i, sc: (sc[1], 0, 0, 0)),
                pl.BlockSpec((1, s, k, share), lambda i, sc: (sc[1], 0, 0, 0)),
                pl.BlockSpec((s, k, 2 * share), fixed3),
            ],
            out_specs=[
                pl.BlockSpec((width, s * k, depth), fixed3),
                pl.BlockSpec((2 * share, s * k), fixed2),
            ],
            scratch_shapes=[
                pltpu.VMEM((width, s * k, depth), f32),
                pltpu.VMEM((k, 2 * k), f32),
            ],
        ),
        out_shape=[
            jax.ShapeDtypeStruct((width, s * k, depth), bf16),
            jax.ShapeDtypeStruct((2 * share, s * k), bf16),
        ],
        compiler_params=pltpu.CompilerParams(vmem_limit_bytes=VMEM),
        cost_estimate=cost(4_000_000_000, 20_000_000),
        name="finish",
    )(scalars, env, site, half, x_site, g_site, x_own, g_own, own, half, site_local)


def summed_over_chips(half):
    return lax.all_to_all(half, CHIPS, 0, 0, tiled=True).astype(f32).sum(axis=0)


def body(
    environment, site_tensor, mpo_tensor, sketch_site, sketch_expand, row_sectors, column_sectors
):
    mpo_index = lax.axis_index(MPO)
    bond_index = lax.axis_index(BOND)
    core = lax.axis_index(CORE)
    chi, width, depth = environment.shape
    local_rows, physical, _ = site_tensor.shape
    columns = column_sectors.shape[1]
    blocks, share = chi // local_rows, local_rows // 2
    mask_rows = sector_mask(row_sectors, column_sectors)
    env = jnp.transpose(environment, (1, 0, 2))
    env_halves = env.reshape(width, blocks, 2, share, depth)
    own_core = core.reshape(1).astype(jnp.int32)
    other_core = 1 - own_core

    site_y = jnp.einsum("asb,bk->ska", site_tensor, sketch_site, preferred_element_type=f32)
    site_local = site_y * jnp.transpose(mask_rows, (1, 2, 0))
    site_all = lax.all_gather(site_local.astype(bf16), BOND, axis=0)

    sketched = jnp.einsum(
        "asb,kwb->wska", site_tensor, sketch_expand, preferred_element_type=f32
    ).astype(bf16)
    applied = jnp.einsum(
        "vwst,wtka->vska", mpo_tensor, sketched, preferred_element_type=f32
    ).astype(bf16)
    contracted = lax.all_to_all(applied, MPO, split_axis=0, concat_axis=2, tiled=True)
    contracted = contracted.reshape(width, physical * columns, depth)

    send = expand_half(other_core, env_halves, contracted)
    got = lax.ppermute(send, CORE, SWAP)
    keep = expand_half(own_core, env_halves, contracted)
    half = (keep.astype(f32) + got.astype(f32)).astype(bf16)
    piece = summed_over_chips(half.reshape(blocks * physical, share, columns))
    mask_piece = lax.dynamic_slice(
        mask_rows, (core * share, lax.axis_index("mpo_0"), 0), (share, 1, columns)
    )[:, 0]
    piece = (piece * mask_piece).T.astype(bf16)
    own = lax.all_to_all(
        jnp.broadcast_to(piece[None], (blocks * physical, columns, share)), CHIPS, 0, 0, tiled=True
    ).reshape(blocks, physical, columns, share)
    other = lax.ppermute(own, CORE, SWAP)

    x_site, g_site = site_terms(env.reshape(width, blocks, local_rows, depth), site_all)
    x_own, g_own = expand_terms(own_core, env_halves, site_all, own)
    scalars = jnp.concatenate([other_core, bond_index.reshape(1).astype(jnp.int32)])
    projected, basis_flat = finish(
        scalars, env_halves, site_all, other, x_site, g_site, x_own, g_own, own, site_local
    )
    basis_local = basis_flat.reshape(local_rows, physical, columns)

    paired = jnp.einsum(
        "wxc,cy->wxy", projected, basis_flat, preferred_element_type=f32
    ).reshape(width, physical, columns, physical, columns)
    operator_rows = lax.dynamic_slice_in_dim(mpo_tensor, mpo_index * width, width, 0)
    share_out = jnp.einsum(
        "wvst,wsktl->kvl", operator_rows.astype(f32), paired, precision=lax.Precision.HIGH
    ).astype(bf16)
    kout, vout = columns // 16, mpo_tensor.shape[1] // 8
    parts = share_out.reshape(16, kout, 4, 2, vout, columns).transpose(3, 0, 2, 1, 4, 5)
    mine = lax.dynamic_index_in_dim(parts, core, 0, keepdims=False)
    sent = lax.dynamic_index_in_dim(parts, 1 - core, 0, keepdims=False)
    both = (mine.astype(f32) + lax.ppermute(sent, CORE, SWAP).astype(f32)).astype(bf16)
    extended = summed_over_chips(both.reshape(64, kout, vout, columns))
    return (basis_local, extended)


def solution(mesh):
    torus = Mesh(mesh.devices.reshape(4, 2, 4, 4), ("mpo_0", "mpo_1", "bond_0", "bond_1"))
    placed = (
        P(None, MPO, BOND),
        P(BOND, None, None),
        P(),
        P(),
        P(MPO, None, None),
        P(None, BOND, None),
        P(),
    )
    return jax.shard_map(
        body,
        mesh=torus,
        in_specs=placed,
        out_specs=(P(BOND, None, None), P(BOND, MPO, None)),
        check_vma=False,
    )
```

```python
import jax
import jax.numpy as jnp
from jax import lax
from jax.experimental import pallas as pl
from jax.experimental.pallas import tpu as pltpu
from jax.sharding import Mesh
from jax.sharding import PartitionSpec as P

MPO = ("mpo_0", "mpo_1")
BOND = ("bond_0", "bond_1")
CHIPS = ("bond_0", "bond_1", "mpo_0")
CORE = "mpo_1"
SWAP = [(0, 1), (1, 0)]

mixing = 0.5
shift_tolerance = 1e-06
f32 = jnp.float32
bf16 = jnp.bfloat16
VMEM = 40 * 1024 * 1024


def sector_mask(row_labels, column_labels):
    match = (row_labels[0][:, :, None] == column_labels[0][None, None, :]) & (
        row_labels[1][:, :, None] == column_labels[1][None, None, :]
    )
    return match.astype(f32)


def dot(a, b, dims):
    return lax.dot_general(a, b, (dims, ((), ())), preferred_element_type=f32)


def cost(flops, size):
    return pl.CostEstimate(flops=flops, bytes_accessed=size, transcendentals=0)


def expand_half(core, env, contracted):
    width, blocks, _, share, depth = env.shape
    x = contracted.shape[1]
    k = share
    s = x // k
    step = 4

    def kernel(core_ref, e_ref, c_ref, o_ref):
        left = jnp.concatenate(
            [e_ref[w, :, 0].reshape(step * share, depth) for w in range(width)], axis=1
        )
        right = jnp.concatenate([c_ref[w] for w in range(width)], axis=1)
        total = dot(left, right, ((1,), (1,)))
        for i in range(s):
            o_ref[:, i] = total[:, i * k : (i + 1) * k].astype(bf16).reshape(step, share, k)

    return pl.pallas_call(
        kernel,
        grid_spec=pltpu.PrefetchScalarGridSpec(
            num_scalar_prefetch=1,
            grid=(blocks // step,),
            in_specs=[
                pl.BlockSpec((width, step, 1, share, depth), lambda i, core: (0, i, core[0], 0, 0)),
                pl.BlockSpec((width, x, depth), lambda i, core: (0, 0, 0)),
            ],
            out_specs=pl.BlockSpec((step, s, share, k), lambda i, core: (i, 0, 0, 0)),
        ),
        out_shape=jax.ShapeDtypeStruct((blocks, s, share, k), bf16),
        compiler_params=pltpu.CompilerParams(vmem_limit_bytes=VMEM),
        cost_estimate=cost(2 * width * blocks * share * depth * x, 9_000_000),
        name="expand_half",
    )(core, env, contracted)


def site_terms(env, site):
    width, blocks, rows, depth = env.shape
    s, k = site.shape[1:3]
    step = 2

    def kernel(e_ref, s_ref, x_ref, g_ref):
        first = pl.program_id(0) == 0
        left = jnp.concatenate([s_ref[z].reshape(s * k, rows) for z in range(step)], axis=1)

        def term(w):
            return dot(left, e_ref[w].reshape(step * rows, depth), ((1,), (0,)))

        wide = jnp.concatenate([left[i * k : (i + 1) * k] for i in range(s)], axis=1)
        gram = dot(wide, wide, ((1,), (1,)))

        @pl.when(first)
        def _():
            for w in range(width):
                x_ref[w] = term(w)
            g_ref[...] = gram

        @pl.when(jnp.logical_not(first))
        def _():
            for w in range(width):
                x_ref[w] += term(w)
            g_ref[...] += gram

    return pl.pallas_call(
        kernel,
        grid=(blocks // step,),
        in_specs=[
            pl.BlockSpec((width, step, rows, depth), lambda i: (0, i, 0, 0)),
            pl.BlockSpec((step, s, k, rows), lambda i: (i, 0, 0, 0)),
        ],
        out_specs=[
            pl.BlockSpec((width, s * k, depth), lambda i: (0, 0, 0)),
            pl.BlockSpec((k, k), lambda i: (0, 0)),
        ],
        out_shape=[
            jax.ShapeDtypeStruct((width, s * k, depth), f32),
            jax.ShapeDtypeStruct((k, k), f32),
        ],
        compiler_params=pltpu.CompilerParams(vmem_limit_bytes=VMEM),
        cost_estimate=cost(6_000_000_000, 17_000_000),
        name="site_terms",
    )(env, site)


def expand_step(e_ref, s_ref, h_ref):
    width, step, _, share, depth = e_ref.shape
    s, k = h_ref.shape[1:3]
    left = jnp.concatenate([h_ref[z].reshape(s * k, share) for z in range(step)], axis=1)
    terms = [
        lambda w=w: dot(left, e_ref[w, :, 0].reshape(step * share, depth), ((1,), (0,)))
        for w in range(width)
    ]
    wide = jnp.concatenate([left[i * k : (i + 1) * k] for i in range(s)], axis=1)
    site = jnp.concatenate([s_ref[z, i] for i in range(s) for z in range(step)], axis=1)
    gram = dot(wide, jnp.concatenate([wide, site], axis=0), ((1,), (1,)))
    return terms, gram


def expand_specs(width, step, share, depth, s, k):
    return [
        pl.BlockSpec((width, step, 1, share, depth), lambda i, sc: (0, i, sc[0], 0, 0)),
        pl.BlockSpec((step, s, k, share), lambda i, sc: (i, 0, 0, sc[0])),
        pl.BlockSpec((step, s, k, share), lambda i, sc: (i, 0, 0, 0)),
    ]


def expand_terms(core, env, site, half):
    width, blocks, _, share, depth = env.shape
    s, k = half.shape[1:3]
    step = 4

    def kernel(core_ref, e_ref, s_ref, h_ref, x_ref, g_ref):
        first = pl.program_id(0) == 0
        terms, gram = expand_step(e_ref, s_ref, h_ref)

        @pl.when(first)
        def _():
            for w in range(width):
                x_ref[w] = terms[w]()
            g_ref[...] = gram

        @pl.when(jnp.logical_not(first))
        def _():
            for w in range(width):
                x_ref[w] += terms[w]()
            g_ref[...] += gram

    return pl.pallas_call(
        kernel,
        grid_spec=pltpu.PrefetchScalarGridSpec(
            num_scalar_prefetch=1,
            grid=(blocks // step,),
            in_specs=expand_specs(width, step, share, depth, s, k),
            out_specs=[
                pl.BlockSpec((width, s * k, depth), lambda i, sc: (0, 0, 0)),
                pl.BlockSpec((k, 2 * k), lambda i, sc: (0, 0)),
            ],
        ),
        out_shape=[
            jax.ShapeDtypeStruct((width, s * k, depth), f32),
            jax.ShapeDtypeStruct((k, 2 * k), f32),
        ],
        compiler_params=pltpu.CompilerParams(vmem_limit_bytes=VMEM),
        cost_estimate=cost(3_300_000_000, 12_000_000),
        name="expand_terms",
    )(core, env, site, half)


def inverse_factor(a, nb):
    n = a.shape[0]
    count = n // 8
    rows = [a[8 * i : 8 * i + 8, :] for i in range(count)]
    lane = lax.broadcasted_iota(jnp.int32, (8, n), 1)
    sub = lax.broadcasted_iota(jnp.int32, (8, n), 0)

    def full(v):
        return jnp.broadcast_to(v, (8, n))

    for j in range(0, n, nb):
        b, o = j // 8, j % 8
        cols = {i: [full(rows[i][:, j + p : j + p + 1]) for p in range(nb)] for i in range(b, count)}
        lines = [full(rows[b][o + q : o + q + 1, :]) for q in range(nb)]
        pivots = [
            [full(cols[b][r][o + q : o + q + 1, :]) for r in range(q + 1)] for q in range(nb)
        ]
        scaled, ratio = [], {}
        for p in range(nb):
            inv = 1.0 / pivots[p][p]
            here = lane == j + p
            line = jnp.where(here, 1.0, lines[p]) * inv
            scaled.append(line)
            for q in range(p + 1, nb):
                ratio[q, p] = pivots[q][p] * inv
            for q in range(p + 1, nb):
                lines[q] = jnp.where(here, 0.0, lines[q]) - pivots[q][p] * line
                for r in range(p + 1, q + 1):
                    pivots[q][r] = pivots[q][r] - pivots[q][p] * ratio[r, p]
        for i in range(b, count):
            c = cols[i]
            value = rows[i]
            for p in range(nb):
                new = jnp.where(lane == j + p, 0.0, value) - c[p] * scaled[p]
                value = jnp.where(sub > o + p, new, value) if i == b else new
                for q in range(p + 1, nb):
                    c[q] = c[q] - c[p] * ratio[q, p]
            rows[i] = value
    w = jnp.concatenate(rows, axis=0)
    row = lax.broadcasted_iota(jnp.int32, (n, n), 0)
    col = lax.broadcasted_iota(jnp.int32, (n, n), 1)
    diagonal = jnp.sum(jnp.where(row == col, w, 0.0), axis=1, keepdims=True)
    unit = jnp.where(row > col, w, 0.0) + jnp.where(row == col, 1.0, 0.0)
    return unit * lax.rsqrt(diagonal)


def split(v):
    high = v.astype(bf16)
    return high, (v - high.astype(f32)).astype(bf16)


def finish(scalars, env, site, half, x_site, g_site, x_own, g_own, own, site_local, operator):
    width, blocks, _, share, depth = env.shape
    s, k = half.shape[1:3]
    step = 4
    last = blocks // step - 1
    pad = operator.shape[0] // 2
    out_rows = pad - 4

    def kernel(
        sc_ref, e_ref, s_ref, h_ref, xs_ref, gs_ref, xo_ref, go_ref, own_ref, oth_ref, sl_ref, m_ref,
        b_ref, give_ref, keep_ref, x_ref, g_ref, p_ref,
    ):
        first = pl.program_id(0) == 0
        terms, gram = expand_step(e_ref, s_ref, h_ref)

        @pl.when(first)
        def _():
            for w in range(width):
                x_ref[w] = xo_ref[w] + terms[w]()
            g_ref[...] = go_ref[...] + gram

        @pl.when(jnp.logical_not(first))
        def _():
            for w in range(width):
                x_ref[w] += terms[w]()
            g_ref[...] += gram

        @pl.when(pl.program_id(0) == last)
        def _():
            gs = gs_ref[...]
            ge = g_ref[:, :k]
            gc = g_ref[:, k:]
            row = lax.broadcasted_iota(jnp.int32, (k, k), 0)
            col = lax.broadcasted_iota(jnp.int32, (k, k), 1)
            trace_site = jnp.sum(jnp.where(row == col, gs, 0.0), keepdims=True)
            trace_expand = jnp.sum(jnp.where(row == col, ge, 0.0), keepdims=True)
            mix = mixing * jnp.sqrt((trace_site + shift_tolerance) / (trace_expand + shift_tolerance))
            inverse = inverse_factor(gs + mix * (gc + gc.T) + (mix * mix) * ge, 8)
            high, low = split(inverse)
            both = jnp.concatenate([high, low], axis=1)

            def apply(v):
                vh, vl = split(v)
                return dot(both, jnp.concatenate([vh, vh], axis=0), ((1,), (0,))) + dot(
                    high, vl, ((1,), (0,))
                )

            for w in range(width):
                for i in range(s):
                    part = slice(i * k, (i + 1) * k)
                    value = apply(xs_ref[w, part] + mix * x_ref[w, part])
                    p_ref[:, pl.ds(w * s + i, k, stride=pad), :] = jnp.stack(
                        [value[:, h * k : (h + 1) * k] for h in range(depth // k)], axis=0
                    )
            for i in range(width * s, pad):
                p_ref[:, pl.ds(i, k, stride=pad), :] = jnp.zeros((depth // k, k, k), f32)
            even = sc_ref[0] == 1
            for i in range(s):
                a0 = own_ref[0, i].astype(f32)
                a1 = oth_ref[0, i].astype(f32)
                rows = jnp.concatenate(
                    [jnp.where(even, a0, a1), jnp.where(even, a1, a0)], axis=1
                )
                done = apply(sl_ref[i] + mix * rows)
                b_ref[:, i * k : (i + 1) * k] = done.T.astype(bf16)

            operator_rows = jnp.concatenate([m_ref[...], m_ref[...]], axis=1)

            def group(g, carry):
                lines = pl.ds(pl.multiple_of(g * (8 * pad), 8 * pad), 8 * pad)
                left = jnp.concatenate(
                    [p_ref[h, lines, :] for h in range(depth // k)], axis=1
                ).astype(bf16)
                paired = dot(left, b_ref[...], ((1,), (0,)))
                for q in range(0, 8, 2):
                    block = jnp.concatenate(
                        [
                            jnp.concatenate(
                                [
                                    paired[r * pad : (r + 1) * pad, t * k : (t + 1) * k]
                                    for t in range(s)
                                ],
                                axis=0,
                            )
                            for r in (q, q + 1)
                        ],
                        axis=1,
                    )
                    bh, bl = split(block)
                    done = dot(operator_rows, jnp.concatenate([bh, bl], axis=0), ((1,), (0,)))
                    for r in (0, 1):
                        piece = done[:, r * k : (r + 1) * k]
                        to = pl.ds(q + r, out_rows, stride=8)
                        give_ref[g, to, :] = piece[:out_rows]
                        keep_ref[g, to, :] = piece[pad : pad + out_rows]
                return carry

            lax.fori_loop(0, k // 8, group, 0)

    fixed3 = lambda i, sc: (0, 0, 0)
    fixed2 = lambda i, sc: (0, 0)
    return pl.pallas_call(
        kernel,
        grid_spec=pltpu.PrefetchScalarGridSpec(
            num_scalar_prefetch=1,
            grid=(blocks // step,),
            in_specs=expand_specs(width, step, share, depth, s, k)
            + [
                pl.BlockSpec((width, s * k, depth), fixed3),
                pl.BlockSpec((k, k), fixed2),
                pl.BlockSpec((width, s * k, depth), fixed3),
                pl.BlockSpec((k, 2 * k), fixed2),
                pl.BlockSpec((1, s, k, share), lambda i, sc: (sc[1], 0, 0, 0)),
                pl.BlockSpec((1, s, k, share), lambda i, sc: (sc[1], 0, 0, 0)),
                pl.BlockSpec((s, k, 2 * share), fixed3),
                pl.BlockSpec(operator.shape, fixed2),
            ],
            out_specs=[
                pl.BlockSpec((2 * share, s * k), fixed2),
                pl.BlockSpec((k // 8, 8 * out_rows, k), fixed3),
                pl.BlockSpec((k // 8, 8 * out_rows, k), fixed3),
            ],
            scratch_shapes=[
                pltpu.VMEM((width, s * k, depth), f32),
                pltpu.VMEM((k, 2 * k), f32),
                pltpu.VMEM((depth // k, k * pad, k), f32),
            ],
        ),
        out_shape=[
            jax.ShapeDtypeStruct((2 * share, s * k), bf16),
            jax.ShapeDtypeStruct((k // 8, 8 * out_rows, k), f32),
            jax.ShapeDtypeStruct((k // 8, 8 * out_rows, k), f32),
        ],
        compiler_params=pltpu.CompilerParams(vmem_limit_bytes=VMEM),
        cost_estimate=cost(4_000_000_000, 20_000_000),
        name="finish",
    )(scalars, env, site, half, x_site, g_site, x_own, g_own, own, half, site_local, operator)


def summed_over_chips(half):
    return lax.all_to_all(half, CHIPS, 0, 0, tiled=True).astype(f32).sum(axis=0)


def body(
    environment, site_tensor, mpo_tensor, sketch_site, sketch_expand, row_sectors, column_sectors
):
    mpo_index = lax.axis_index(MPO)
    bond_index = lax.axis_index(BOND)
    core = lax.axis_index(CORE)
    chi, width, depth = environment.shape
    local_rows, physical, _ = site_tensor.shape
    columns = column_sectors.shape[1]
    blocks, share = chi // local_rows, local_rows // 2
    mask_rows = sector_mask(row_sectors, column_sectors)
    env = jnp.transpose(environment, (1, 0, 2))
    env_halves = env.reshape(width, blocks, 2, share, depth)
    own_core = core.reshape(1).astype(jnp.int32)
    other_core = 1 - own_core

    operator = lax.dynamic_slice_in_dim(mpo_tensor, mpo_index * width, width, 0)
    operator = jnp.transpose(operator.reshape(width, 4, 2, -1, physical, physical), (2, 1, 3, 5, 0, 4))
    operator = operator.reshape(2, -1, physical, width * physical)
    operator = jnp.pad(operator, ((0, 0), (0, 4), (0, 0), (0, 4)))
    operator = jnp.where(core == 0, operator[::-1], operator).reshape(2 * operator.shape[1], -1)

    sketched = jnp.einsum(
        "asb,kwb->wska", site_tensor, sketch_expand, preferred_element_type=f32
    ).astype(bf16)
    applied = jnp.einsum(
        "vwst,wtka->vska", mpo_tensor, sketched, preferred_element_type=f32
    ).astype(bf16)
    applied, sketch_site = lax.optimization_barrier((applied, sketch_site))
    site_y = jnp.einsum("asb,bk->ska", site_tensor, sketch_site, preferred_element_type=f32)
    site_local = site_y * jnp.transpose(mask_rows, (1, 2, 0))
    site_all = lax.all_gather(site_local.astype(bf16), BOND, axis=0)
    contracted = lax.all_to_all(applied, MPO, split_axis=0, concat_axis=2, tiled=True)
    contracted, site_local = lax.optimization_barrier((contracted, site_local))
    contracted = contracted.reshape(width, physical * columns, depth)

    send = expand_half(other_core, env_halves, contracted)
    got = lax.ppermute(send, CORE, SWAP)
    keep = expand_half(own_core, env_halves, contracted)
    half = (keep.astype(f32) + got.astype(f32)).astype(bf16)
    x_site, g_site = site_terms(env.reshape(width, blocks, local_rows, depth), site_all)
    arrived = lax.all_to_all(half.reshape(-1, share, columns), CHIPS, 0, 0, tiled=True)
    arrived, x_site, g_site = lax.optimization_barrier((arrived, x_site, g_site))
    piece = arrived.astype(f32).sum(axis=0)
    mask_piece = lax.dynamic_slice(
        mask_rows, (core * share, lax.axis_index("mpo_0"), 0), (share, 1, columns)
    )[:, 0]
    piece = (piece * mask_piece).T.astype(bf16)
    own = lax.all_to_all(
        jnp.broadcast_to(piece[None], (blocks * physical, columns, share)), CHIPS, 0, 0, tiled=True
    ).reshape(blocks, physical, columns, share)
    other = lax.ppermute(own, CORE, SWAP)

    x_own, g_own = expand_terms(own_core, env_halves, site_all, own)
    scalars = jnp.concatenate([other_core, bond_index.reshape(1).astype(jnp.int32)])
    basis_flat, give, kept = finish(
        scalars, env_halves, site_all, other, x_site, g_site, x_own, g_own, own, site_local, operator
    )
    basis_local = basis_flat.reshape(local_rows, physical, columns)

    both = (kept + lax.ppermute(give, CORE, SWAP)).astype(bf16)
    chips = blocks * physical
    extended = summed_over_chips(both.reshape(chips, -1, columns))
    extended = jnp.swapaxes(extended.reshape(-1, 8, columns), 0, 1)
    return (basis_local, extended)


def solution(mesh):
    torus = Mesh(mesh.devices.reshape(4, 2, 4, 4), ("mpo_0", "mpo_1", "bond_0", "bond_1"))
    placed = (
        P(None, MPO, BOND),
        P(BOND, None, None),
        P(),
        P(),
        P(MPO, None, None),
        P(None, BOND, None),
        P(),
    )
    return jax.shard_map(
        body,
        mesh=torus,
        in_specs=placed,
        out_specs=(P(BOND, None, None), P(BOND, MPO, None)),
        check_vma=False,
    )
```

```python
import jax
import jax.numpy as jnp
from jax import lax
from jax.experimental import pallas as pl
from jax.experimental.pallas import tpu as pltpu
from jax.sharding import Mesh
from jax.sharding import PartitionSpec as P

MPO = ("mpo_0", "mpo_1")
BOND = ("bond_0", "bond_1")
CHIPS = ("bond_0", "bond_1", "mpo_0")
CORE = "mpo_1"
SWAP = [(0, 1), (1, 0)]

mixing = 0.5
shift_tolerance = 1e-06
f32 = jnp.float32
bf16 = jnp.bfloat16
MIB = 1024 * 1024


def sector_mask(row_labels, column_labels):
    match = (row_labels[0][:, :, None] == column_labels[0][None, None, :]) & (
        row_labels[1][:, :, None] == column_labels[1][None, None, :]
    )
    return match.astype(f32)


def dot(a, b, dims):
    return lax.dot_general(a, b, (dims, ((), ())), preferred_element_type=f32)


def in_hbm(value):
    return pltpu.with_memory_space_constraint(value, pltpu.HBM)


def cost(flops, size):
    return pl.CostEstimate(flops=flops, bytes_accessed=size, transcendentals=0)


def sketch(site_tensor, sketch_expand, sketch_site, width):
    rows, s, depth = site_tensor.shape
    k, v, _ = sketch_expand.shape
    columns = sketch_site.shape[1]
    share = 128
    halves, lines = rows // share, share * s
    last = depth // width - 1

    def kernel(s_ref, o_ref, w_ref, y_ref, z_ref, total, site_total):
        step = pl.program_id(0)
        expand = o_ref[...].reshape(k * v, width)
        for h in range(halves):
            block = s_ref[h * share : (h + 1) * share].reshape(lines, width)

            @pl.when(step == 0)
            def _():
                total[h] = dot(expand, block, ((1,), (1,)))
                site_total[h] = dot(block, w_ref[...], ((1,), (0,)))

            @pl.when(step > 0)
            def _():
                total[h] += dot(expand, block, ((1,), (1,)))
                site_total[h] += dot(block, w_ref[...], ((1,), (0,)))

        @pl.when(step == last)
        def _():
            row = lax.broadcasted_iota(jnp.int32, (lines, lines), 0)
            col = lax.broadcasted_iota(jnp.int32, (lines, lines), 1)
            order = jnp.where((row % s) * share + row // s == col, 1.0, 0.0).astype(bf16)
            for h in range(halves):
                to = slice(h * share, (h + 1) * share)
                y = dot(total[h].astype(bf16), order, ((1,), (0,))).astype(bf16)
                for i in range(k):
                    for t in range(s):
                        y_ref[i, t, :, to] = y[i * v : (i + 1) * v, t * share : (t + 1) * share]
                high, low = split(site_total[h].T)
                z = dot(jnp.concatenate([high, low], axis=0), order, ((1,), (0,)))
                z = z[:columns] + z[columns:]
                for t in range(s):
                    z_ref[t, :, to] = z[:, t * share : (t + 1) * share]

    return pl.pallas_call(
        kernel,
        grid=(last + 1,),
        in_specs=[
            pl.BlockSpec((rows, s, width), lambda i: (0, 0, i)),
            pl.BlockSpec((k, v, width), lambda i: (0, 0, i)),
            pl.BlockSpec((width, columns), lambda i: (i, 0)),
        ],
        out_specs=[
            pl.BlockSpec((k, s, v, rows), lambda i: (0, 0, 0, 0)),
            pl.BlockSpec((s, columns, rows), lambda i: (0, 0, 0)),
        ],
        out_shape=[
            jax.ShapeDtypeStruct((k, s, v, rows), bf16),
            jax.ShapeDtypeStruct((s, columns, rows), f32),
        ],
        scratch_shapes=[
            pltpu.VMEM((halves, k * v, lines), f32),
            pltpu.VMEM((halves, lines, columns), f32),
        ],
        compiler_params=pltpu.CompilerParams(vmem_limit_bytes=36 * MIB),
        cost_estimate=cost(7_000_000_000, 15_000_000),
        name="sketch",
    )(in_hbm(site_tensor), in_hbm(sketch_expand), in_hbm(sketch_site))


def expand_half(core, env, contracted):
    width, blocks, _, share, depth = env.shape
    x = contracted.shape[1]
    k = share
    s = x // k
    step = 4
    steps = blocks // step

    def kernel(core_ref, e_ref, c_ref, o_ref, near, sem):
        core = core_ref[0]
        copies = [
            pltpu.make_async_copy(
                e_ref.at[:, pl.ds(i * step, step), core],
                near.at[:, pl.ds(i * step, step)],
                sem.at[i],
            )
            for i in range(steps)
        ]
        for copy in copies:
            copy.start()
        right = jnp.concatenate([c_ref[w] for w in range(width)], axis=1)
        for i in range(steps):
            copies[i].wait()
            n = pl.ds(i * step, step)
            left = jnp.concatenate(
                [near[w, n].reshape(step * share, depth) for w in range(width)], axis=1
            )
            total = dot(left, right, ((1,), (1,)))
            for t in range(s):
                o_ref[n, t] = total[:, t * k : (t + 1) * k].astype(bf16).reshape(step, share, k)

    return pl.pallas_call(
        kernel,
        in_specs=[
            pl.BlockSpec(memory_space=pltpu.SMEM),
            pl.BlockSpec(memory_space=pl.ANY),
            pl.BlockSpec(memory_space=pltpu.VMEM),
        ],
        out_specs=pl.BlockSpec(memory_space=pltpu.VMEM),
        out_shape=jax.ShapeDtypeStruct((blocks, s, share, k), bf16),
        scratch_shapes=[
            pltpu.VMEM((width, blocks, share, depth), bf16),
            pltpu.SemaphoreType.DMA((steps,)),
        ],
        compiler_params=pltpu.CompilerParams(vmem_limit_bytes=24 * MIB),
        cost_estimate=cost(2 * width * blocks * share * depth * x, 9_000_000),
        name="expand_half",
    )(core, in_hbm(env), contracted)


def site_terms(env, site):
    width, blocks, _, share, depth = env.shape
    rows = 2 * share
    s, k = site.shape[1:3]
    step = 2

    def kernel(e_ref, s_ref, x_ref, g_ref):
        first = pl.program_id(0) == 0
        left = jnp.concatenate([s_ref[z].reshape(s * k, rows) for z in range(step)], axis=1)

        def term(w):
            return dot(left, e_ref[w].reshape(step * rows, depth), ((1,), (0,)))

        wide = jnp.concatenate([left[i * k : (i + 1) * k] for i in range(s)], axis=1)
        gram = dot(wide, wide, ((1,), (1,)))

        @pl.when(first)
        def _():
            for w in range(width):
                x_ref[w] = term(w)
            g_ref[...] = gram

        @pl.when(jnp.logical_not(first))
        def _():
            for w in range(width):
                x_ref[w] += term(w)
            g_ref[...] += gram

    return pl.pallas_call(
        kernel,
        grid=(blocks // step,),
        in_specs=[
            pl.BlockSpec((width, step, 2, share, depth), lambda i: (0, i, 0, 0, 0)),
            pl.BlockSpec((step, s, k, rows), lambda i: (i, 0, 0, 0)),
        ],
        out_specs=[
            pl.BlockSpec((width, s * k, depth), lambda i: (0, 0, 0)),
            pl.BlockSpec((k, k), lambda i: (0, 0)),
        ],
        out_shape=[
            jax.ShapeDtypeStruct((width, s * k, depth), f32),
            jax.ShapeDtypeStruct((k, k), f32),
        ],
        compiler_params=pltpu.CompilerParams(vmem_limit_bytes=20 * MIB),
        cost_estimate=cost(6_000_000_000, 17_000_000),
        name="site_terms",
    )(in_hbm(env), in_hbm(site))


def expand_step(e_ref, s_ref, h_ref):
    width, _, _, share, depth = e_ref.shape
    step, s, k = h_ref.shape[:3]
    left = jnp.concatenate([h_ref[z].reshape(s * k, share) for z in range(step)], axis=1)
    terms = [
        lambda w=w: dot(left, e_ref[w, :, 0].reshape(step * share, depth), ((1,), (0,)))
        for w in range(width)
    ]
    wide = jnp.concatenate([left[i * k : (i + 1) * k] for i in range(s)], axis=1)
    site = jnp.concatenate([s_ref[z, i] for i in range(s) for z in range(step)], axis=1)
    gram = dot(wide, jnp.concatenate([wide, site], axis=0), ((1,), (1,)))
    return terms, gram


def expand_specs(width, step, share, depth, s, k):
    return [
        pl.BlockSpec((width, step, 1, share, depth), lambda i, sc: (0, i, sc[0], 0, 0)),
        pl.BlockSpec((step, s, k, share), lambda i, sc: (i, 0, 0, sc[0])),
        pl.BlockSpec((step, s, k, share), lambda i, sc: (i, 0, 0, 0)),
    ]


def expand_terms(core, env, site, half):
    width, blocks, _, share, depth = env.shape
    s, k = half.shape[1:3]
    step = 4

    def kernel(core_ref, e_ref, s_ref, h_ref, x_ref, g_ref):
        first = pl.program_id(0) == 0
        terms, gram = expand_step(e_ref, s_ref, h_ref)

        @pl.when(first)
        def _():
            for w in range(width):
                x_ref[w] = terms[w]()
            g_ref[...] = gram

        @pl.when(jnp.logical_not(first))
        def _():
            for w in range(width):
                x_ref[w] += terms[w]()
            g_ref[...] += gram

    return pl.pallas_call(
        kernel,
        grid_spec=pltpu.PrefetchScalarGridSpec(
            num_scalar_prefetch=1,
            grid=(blocks // step,),
            in_specs=expand_specs(width, step, share, depth, s, k),
            out_specs=[
                pl.BlockSpec((width, s * k, depth), lambda i, sc: (0, 0, 0)),
                pl.BlockSpec((k, 2 * k), lambda i, sc: (0, 0)),
            ],
        ),
        out_shape=[
            jax.ShapeDtypeStruct((width, s * k, depth), f32),
            jax.ShapeDtypeStruct((k, 2 * k), f32),
        ],
        compiler_params=pltpu.CompilerParams(vmem_limit_bytes=20 * MIB),
        cost_estimate=cost(3_300_000_000, 12_000_000),
        name="expand_terms",
    )(core, in_hbm(env), in_hbm(site), half)


def inverse_factor(a, nb):
    n = a.shape[0]
    count = n // 8
    rows = [a[8 * i : 8 * i + 8, :] for i in range(count)]
    lane = lax.broadcasted_iota(jnp.int32, (8, n), 1)
    sub = lax.broadcasted_iota(jnp.int32, (8, n), 0)

    def full(v):
        return jnp.broadcast_to(v, (8, n))

    for j in range(0, n, nb):
        b, o = j // 8, j % 8
        cols = {i: [full(rows[i][:, j + p : j + p + 1]) for p in range(nb)] for i in range(b, count)}
        lines = [full(rows[b][o + q : o + q + 1, :]) for q in range(nb)]
        pivots = [
            [full(cols[b][r][o + q : o + q + 1, :]) for r in range(q + 1)] for q in range(nb)
        ]
        scaled, ratio = [], {}
        for p in range(nb):
            inv = 1.0 / pivots[p][p]
            here = lane == j + p
            line = jnp.where(here, 1.0, lines[p]) * inv
            scaled.append(line)
            for q in range(p + 1, nb):
                ratio[q, p] = pivots[q][p] * inv
            for q in range(p + 1, nb):
                lines[q] = jnp.where(here, 0.0, lines[q]) - pivots[q][p] * line
                for r in range(p + 1, q + 1):
                    pivots[q][r] = pivots[q][r] - pivots[q][p] * ratio[r, p]
        for i in range(b, count):
            c = cols[i]
            value = rows[i]
            for p in range(nb):
                new = jnp.where(lane == j + p, 0.0, value) - c[p] * scaled[p]
                value = jnp.where(sub > o + p, new, value) if i == b else new
                for q in range(p + 1, nb):
                    c[q] = c[q] - c[p] * ratio[q, p]
            rows[i] = value
    w = jnp.concatenate(rows, axis=0)
    row = lax.broadcasted_iota(jnp.int32, (n, n), 0)
    col = lax.broadcasted_iota(jnp.int32, (n, n), 1)
    diagonal = jnp.sum(jnp.where(row == col, w, 0.0), axis=1, keepdims=True)
    unit = jnp.where(row > col, w, 0.0) + jnp.where(row == col, 1.0, 0.0)
    return unit * lax.rsqrt(diagonal)


def split(v):
    high = v.astype(bf16)
    return high, (v - high.astype(f32)).astype(bf16)


def finish(scalars, env, site, half, x_site, g_site, x_own, g_own, own, site_local, operator):
    width, blocks, _, share, depth = env.shape
    s, k = half.shape[1:3]
    step = 4
    last = blocks // step - 1
    pad = operator.shape[0] // 2
    out_rows = pad - 4

    def kernel(
        sc_ref, e_ref, s_ref, h_ref, xs_ref, gs_ref, xo_ref, go_ref, own_ref, oth_ref, sl_ref, m_ref,
        b_ref, give_ref, keep_ref, x_ref, g_ref, p_ref,
    ):
        first = pl.program_id(0) == 0
        terms, gram = expand_step(e_ref, s_ref, h_ref)

        @pl.when(first)
        def _():
            for w in range(width):
                x_ref[w] = xo_ref[w] + terms[w]()
            g_ref[...] = go_ref[...] + gram

        @pl.when(jnp.logical_not(first))
        def _():
            for w in range(width):
                x_ref[w] += terms[w]()
            g_ref[...] += gram

        @pl.when(pl.program_id(0) == last)
        def _():
            gs = gs_ref[...]
            ge = g_ref[:, :k]
            gc = g_ref[:, k:]
            row = lax.broadcasted_iota(jnp.int32, (k, k), 0)
            col = lax.broadcasted_iota(jnp.int32, (k, k), 1)
            trace_site = jnp.sum(jnp.where(row == col, gs, 0.0), keepdims=True)
            trace_expand = jnp.sum(jnp.where(row == col, ge, 0.0), keepdims=True)
            mix = mixing * jnp.sqrt((trace_site + shift_tolerance) / (trace_expand + shift_tolerance))
            inverse = inverse_factor(gs + mix * (gc + gc.T) + (mix * mix) * ge, 8)
            high, low = split(inverse)
            both = jnp.concatenate([high, low], axis=1)

            def apply(v):
                vh, vl = split(v)
                return dot(both, jnp.concatenate([vh, vh], axis=0), ((1,), (0,))) + dot(
                    high, vl, ((1,), (0,))
                )

            for w in range(width):
                for i in range(s):
                    part = slice(i * k, (i + 1) * k)
                    value = apply(xs_ref[w, part] + mix * x_ref[w, part])
                    p_ref[:, pl.ds(w * s + i, k, stride=pad), :] = jnp.stack(
                        [value[:, h * k : (h + 1) * k] for h in range(depth // k)], axis=0
                    )
            for i in range(width * s, pad):
                p_ref[:, pl.ds(i, k, stride=pad), :] = jnp.zeros((depth // k, k, k), f32)
            even = sc_ref[0] == 1
            for i in range(s):
                a0 = own_ref[0, i].astype(f32)
                a1 = oth_ref[0, i].astype(f32)
                rows = jnp.concatenate(
                    [jnp.where(even, a0, a1), jnp.where(even, a1, a0)], axis=1
                )
                done = apply(sl_ref[i] + mix * rows)
                b_ref[:, i * k : (i + 1) * k] = done.T.astype(bf16)

            operator_rows = jnp.concatenate([m_ref[...], m_ref[...]], axis=1)

            def group(g, carry):
                lines = pl.ds(pl.multiple_of(g * (8 * pad), 8 * pad), 8 * pad)
                left = jnp.concatenate(
                    [p_ref[h, lines, :] for h in range(depth // k)], axis=1
                ).astype(bf16)
                paired = dot(left, b_ref[...], ((1,), (0,)))
                for q in range(0, 8, 2):
                    block = jnp.concatenate(
                        [
                            jnp.concatenate(
                                [
                                    paired[r * pad : (r + 1) * pad, t * k : (t + 1) * k]
                                    for t in range(s)
                                ],
                                axis=0,
                            )
                            for r in (q, q + 1)
                        ],
                        axis=1,
                    )
                    bh, bl = split(block)
                    done = dot(operator_rows, jnp.concatenate([bh, bl], axis=0), ((1,), (0,)))
                    for r in (0, 1):
                        piece = done[:, r * k : (r + 1) * k]
                        to = pl.ds(q + r, out_rows, stride=8)
                        give_ref[g, to, :] = piece[:out_rows]
                        keep_ref[g, to, :] = piece[pad : pad + out_rows]
                return carry

            lax.fori_loop(0, k // 8, group, 0)

    fixed3 = lambda i, sc: (0, 0, 0)
    fixed2 = lambda i, sc: (0, 0)
    return pl.pallas_call(
        kernel,
        grid_spec=pltpu.PrefetchScalarGridSpec(
            num_scalar_prefetch=1,
            grid=(blocks // step,),
            in_specs=expand_specs(width, step, share, depth, s, k)
            + [
                pl.BlockSpec((width, s * k, depth), fixed3),
                pl.BlockSpec((k, k), fixed2),
                pl.BlockSpec((width, s * k, depth), fixed3),
                pl.BlockSpec((k, 2 * k), fixed2),
                pl.BlockSpec((1, s, k, share), lambda i, sc: (sc[1], 0, 0, 0)),
                pl.BlockSpec((1, s, k, share), lambda i, sc: (sc[1], 0, 0, 0)),
                pl.BlockSpec((s, k, 2 * share), fixed3),
                pl.BlockSpec(operator.shape, fixed2),
            ],
            out_specs=[
                pl.BlockSpec((2 * share, s * k), fixed2),
                pl.BlockSpec((k // 8, 8 * out_rows, k), fixed3),
                pl.BlockSpec((k // 8, 8 * out_rows, k), fixed3),
            ],
            scratch_shapes=[
                pltpu.VMEM((width, s * k, depth), f32),
                pltpu.VMEM((k, 2 * k), f32),
                pltpu.VMEM((depth // k, k * pad, k), f32),
            ],
        ),
        out_shape=[
            jax.ShapeDtypeStruct((2 * share, s * k), bf16),
            jax.ShapeDtypeStruct((k // 8, 8 * out_rows, k), f32),
            jax.ShapeDtypeStruct((k // 8, 8 * out_rows, k), f32),
        ],
        compiler_params=pltpu.CompilerParams(vmem_limit_bytes=36 * MIB),
        cost_estimate=cost(4_000_000_000, 20_000_000),
        name="finish",
    )(scalars, in_hbm(env), in_hbm(site), half, x_site, g_site, x_own, g_own, own, half, site_local, operator)


def summed_over_chips(half):
    return lax.all_to_all(half, CHIPS, 0, 0, tiled=True).astype(f32).sum(axis=0)


def body(
    environment, site_tensor, mpo_tensor, sketch_site, sketch_expand, row_sectors, column_sectors
):
    mpo_index = lax.axis_index(MPO)
    bond_index = lax.axis_index(BOND)
    core = lax.axis_index(CORE)
    chi, width, depth = environment.shape
    local_rows, physical, _ = site_tensor.shape
    columns = column_sectors.shape[1]
    blocks, share = chi // local_rows, local_rows // 2
    mask_rows = sector_mask(row_sectors, column_sectors)
    env = jnp.transpose(environment, (1, 0, 2)).reshape(width, blocks, 2, share, depth)
    own_core = core.reshape(1).astype(jnp.int32)
    other_core = 1 - own_core

    operator = lax.dynamic_slice_in_dim(mpo_tensor, mpo_index * width, width, 0)
    operator = jnp.transpose(operator.reshape(width, 4, 2, -1, physical, physical), (2, 1, 3, 5, 0, 4))
    operator = operator.reshape(2, -1, physical, width * physical)
    operator = jnp.pad(operator, ((0, 0), (0, 4), (0, 0), (0, 4)))
    operator = jnp.where(core == 0, operator[::-1], operator).reshape(2 * operator.shape[1], -1)

    sketched, site_y = sketch(site_tensor, sketch_expand, sketch_site, 1024)
    site_local = site_y * jnp.transpose(mask_rows, (1, 2, 0))
    site_all = lax.all_gather(site_local.astype(bf16), BOND, axis=0)
    applied = jnp.einsum(
        "vwst,ktwa->vska", mpo_tensor, sketched, preferred_element_type=f32
    ).astype(bf16)
    contracted = lax.all_to_all(applied, MPO, split_axis=0, concat_axis=2, tiled=True)
    contracted = contracted.reshape(width, physical * columns, depth)

    send = expand_half(other_core, env, contracted)
    got = lax.ppermute(send, CORE, SWAP)
    keep = expand_half(own_core, env, contracted)
    half = (keep.astype(f32) + got.astype(f32)).astype(bf16)
    x_site, g_site = site_terms(env, site_all)
    arrived = lax.all_to_all(half.reshape(-1, share, columns), CHIPS, 0, 0, tiled=True)
    arrived, x_site, g_site = lax.optimization_barrier((arrived, x_site, g_site))
    piece = arrived.astype(f32).sum(axis=0)
    mask_piece = lax.dynamic_slice(
        mask_rows, (core * share, lax.axis_index("mpo_0"), 0), (share, 1, columns)
    )[:, 0]
    piece = (piece * mask_piece).T.astype(bf16)
    own = lax.all_to_all(
        jnp.broadcast_to(piece[None], (blocks * physical, columns, share)), CHIPS, 0, 0, tiled=True
    ).reshape(blocks, physical, columns, share)
    other = lax.ppermute(own, CORE, SWAP)

    x_own, g_own = expand_terms(own_core, env, site_all, own)
    scalars = jnp.concatenate([other_core, bond_index.reshape(1).astype(jnp.int32)])
    basis_flat, give, kept = finish(
        scalars, env, site_all, other, x_site, g_site, x_own, g_own, own, site_local, operator
    )
    basis_local = basis_flat.reshape(local_rows, physical, columns)

    both = (kept + lax.ppermute(give, CORE, SWAP)).astype(bf16)
    chips = blocks * physical
    extended = summed_over_chips(both.reshape(chips, -1, columns))
    extended = jnp.swapaxes(extended.reshape(-1, 8, columns), 0, 1)
    return (basis_local, extended)


def solution(mesh):
    torus = Mesh(mesh.devices.reshape(4, 2, 4, 4), ("mpo_0", "mpo_1", "bond_0", "bond_1"))
    placed = (
        P(None, MPO, BOND),
        P(BOND, None, None),
        P(),
        P(),
        P(MPO, None, None),
        P(None, BOND, None),
        P(),
    )
    return jax.shard_map(
        body,
        mesh=torus,
        in_specs=placed,
        out_specs=(P(BOND, None, None), P(BOND, MPO, None)),
        check_vma=False,
    )
```

```python
import jax
import jax.numpy as jnp
from jax import lax
from jax.experimental import pallas as pl
from jax.experimental.pallas import tpu as pltpu
from jax.sharding import Mesh
from jax.sharding import PartitionSpec as P

MPO = ("mpo_0", "mpo_1")
BOND = ("bond_0", "bond_1")
CHIPS = ("bond_0", "bond_1", "mpo_0")
CORE = "mpo_1"
SWAP = [(0, 1), (1, 0)]

mixing = 0.5
shift_tolerance = 1e-06
f32 = jnp.float32
bf16 = jnp.bfloat16
MIB = 1024 * 1024


def sector_mask(row_labels, column_labels):
    match = (row_labels[0][:, :, None] == column_labels[0][None, None, :]) & (
        row_labels[1][:, :, None] == column_labels[1][None, None, :]
    )
    return match.astype(f32)


def dot(a, b, dims):
    return lax.dot_general(a, b, (dims, ((), ())), preferred_element_type=f32)


def in_hbm(value):
    return pltpu.with_memory_space_constraint(value, pltpu.HBM)


def cost(flops, size):
    return pl.CostEstimate(flops=flops, bytes_accessed=size, transcendentals=0)


def sketch(site_tensor, sketch_expand, sketch_site, width):
    rows, s, depth = site_tensor.shape
    k, v, _ = sketch_expand.shape
    columns = sketch_site.shape[1]
    share = 128
    halves, lines = rows // share, share * s
    last = depth // width - 1

    def kernel(s_ref, o_ref, w_ref, y_ref, z_ref, total, site_total):
        step = pl.program_id(0)
        expand = o_ref[...].reshape(k * v, width)
        for h in range(halves):
            block = s_ref[h * share : (h + 1) * share].reshape(lines, width)

            @pl.when(step == 0)
            def _():
                total[h] = dot(expand, block, ((1,), (1,)))
                site_total[h] = dot(block, w_ref[...], ((1,), (0,)))

            @pl.when(step > 0)
            def _():
                total[h] += dot(expand, block, ((1,), (1,)))
                site_total[h] += dot(block, w_ref[...], ((1,), (0,)))

        @pl.when(step == last)
        def _():
            row = lax.broadcasted_iota(jnp.int32, (lines, lines), 0)
            col = lax.broadcasted_iota(jnp.int32, (lines, lines), 1)
            order = jnp.where((row % s) * share + row // s == col, 1.0, 0.0).astype(bf16)
            for h in range(halves):
                to = slice(h * share, (h + 1) * share)
                y = dot(total[h].astype(bf16), order, ((1,), (0,))).astype(bf16)
                for i in range(k):
                    for t in range(s):
                        y_ref[i, t, :, to] = y[i * v : (i + 1) * v, t * share : (t + 1) * share]
                high, low = split(site_total[h].T)
                z = dot(jnp.concatenate([high, low], axis=0), order, ((1,), (0,)))
                z = z[:columns] + z[columns:]
                for t in range(s):
                    z_ref[t, :, to] = z[:, t * share : (t + 1) * share]

    return pl.pallas_call(
        kernel,
        grid=(last + 1,),
        in_specs=[
            pl.BlockSpec((rows, s, width), lambda i: (0, 0, i)),
            pl.BlockSpec((k, v, width), lambda i: (0, 0, i)),
            pl.BlockSpec((width, columns), lambda i: (i, 0)),
        ],
        out_specs=[
            pl.BlockSpec((k, s, v, rows), lambda i: (0, 0, 0, 0)),
            pl.BlockSpec((s, columns, rows), lambda i: (0, 0, 0)),
        ],
        out_shape=[
            jax.ShapeDtypeStruct((k, s, v, rows), bf16),
            jax.ShapeDtypeStruct((s, columns, rows), f32),
        ],
        scratch_shapes=[
            pltpu.VMEM((halves, k * v, lines), f32),
            pltpu.VMEM((halves, lines, columns), f32),
        ],
        compiler_params=pltpu.CompilerParams(vmem_limit_bytes=36 * MIB),
        cost_estimate=cost(7_000_000_000, 15_000_000),
        name="sketch",
    )(in_hbm(site_tensor), in_hbm(sketch_expand), in_hbm(sketch_site))


def expand_half(core, env, contracted):
    width, blocks, _, share, depth = env.shape
    x = contracted.shape[1]
    k = share
    s = x // k
    step = 4
    steps = blocks // step

    def kernel(core_ref, e_ref, c_ref, o_ref, near, sem):
        core = core_ref[0]
        copies = [
            pltpu.make_async_copy(
                e_ref.at[:, pl.ds(i * step, step), core],
                near.at[:, pl.ds(i * step, step)],
                sem.at[i],
            )
            for i in range(steps)
        ]
        for copy in copies:
            copy.start()
        right = jnp.concatenate([c_ref[w] for w in range(width)], axis=1)
        for i in range(steps):
            copies[i].wait()
            n = pl.ds(i * step, step)
            left = jnp.concatenate(
                [near[w, n].reshape(step * share, depth) for w in range(width)], axis=1
            )
            total = dot(left, right, ((1,), (1,)))
            for t in range(s):
                o_ref[n, t] = total[:, t * k : (t + 1) * k].astype(bf16).reshape(step, share, k)

    return pl.pallas_call(
        kernel,
        in_specs=[
            pl.BlockSpec(memory_space=pltpu.SMEM),
            pl.BlockSpec(memory_space=pl.ANY),
            pl.BlockSpec(memory_space=pltpu.VMEM),
        ],
        out_specs=pl.BlockSpec(memory_space=pltpu.VMEM),
        out_shape=jax.ShapeDtypeStruct((blocks, s, share, k), bf16),
        scratch_shapes=[
            pltpu.VMEM((width, blocks, share, depth), bf16),
            pltpu.SemaphoreType.DMA((steps,)),
        ],
        compiler_params=pltpu.CompilerParams(vmem_limit_bytes=24 * MIB),
        cost_estimate=cost(2 * width * blocks * share * depth * x, 9_000_000),
        name="expand_half",
    )(core, in_hbm(env), contracted)


def site_terms(env, site):
    width, blocks, _, share, depth = env.shape
    rows = 2 * share
    s, k = site.shape[1:3]
    step = 2

    def kernel(e_ref, s_ref, x_ref, g_ref):
        first = pl.program_id(0) == 0
        left = jnp.concatenate([s_ref[z].reshape(s * k, rows) for z in range(step)], axis=1)

        def term(w):
            return dot(left, e_ref[w].reshape(step * rows, depth), ((1,), (0,)))

        wide = jnp.concatenate([left[i * k : (i + 1) * k] for i in range(s)], axis=1)
        gram = dot(wide, wide, ((1,), (1,)))

        @pl.when(first)
        def _():
            for w in range(width):
                x_ref[w] = term(w)
            g_ref[...] = gram

        @pl.when(jnp.logical_not(first))
        def _():
            for w in range(width):
                x_ref[w] += term(w)
            g_ref[...] += gram

    return pl.pallas_call(
        kernel,
        grid=(blocks // step,),
        in_specs=[
            pl.BlockSpec((width, step, 2, share, depth), lambda i: (0, i, 0, 0, 0)),
            pl.BlockSpec((step, s, k, rows), lambda i: (i, 0, 0, 0)),
        ],
        out_specs=[
            pl.BlockSpec((width, s * k, depth), lambda i: (0, 0, 0)),
            pl.BlockSpec((k, k), lambda i: (0, 0)),
        ],
        out_shape=[
            jax.ShapeDtypeStruct((width, s * k, depth), f32),
            jax.ShapeDtypeStruct((k, k), f32),
        ],
        compiler_params=pltpu.CompilerParams(vmem_limit_bytes=20 * MIB),
        cost_estimate=cost(6_000_000_000, 17_000_000),
        name="site_terms",
    )(in_hbm(env), in_hbm(site))


def expand_step(e_ref, s_ref, h_ref):
    width, _, _, share, depth = e_ref.shape
    step, s, k = h_ref.shape[:3]
    left = jnp.concatenate([h_ref[z].reshape(s * k, share) for z in range(step)], axis=1)
    terms = [
        lambda w=w: dot(left, e_ref[w, :, 0].reshape(step * share, depth), ((1,), (0,)))
        for w in range(width)
    ]
    wide = jnp.concatenate([left[i * k : (i + 1) * k] for i in range(s)], axis=1)
    site = jnp.concatenate([s_ref[z, i] for i in range(s) for z in range(step)], axis=1)
    gram = dot(wide, jnp.concatenate([wide, site], axis=0), ((1,), (1,)))
    return terms, gram


def expand_specs(width, step, share, depth, s, k):
    return [
        pl.BlockSpec((width, step, 1, share, depth), lambda i, sc: (0, i, sc[0], 0, 0)),
        pl.BlockSpec((step, s, k, share), lambda i, sc: (i, 0, 0, sc[0])),
        pl.BlockSpec((step, s, k, share), lambda i, sc: (i, 0, 0, 0)),
    ]


def expand_terms(core, env, site, half):
    width, blocks, _, share, depth = env.shape
    s, k = half.shape[1:3]
    step = 4

    def kernel(core_ref, e_ref, s_ref, h_ref, x_ref, g_ref):
        first = pl.program_id(0) == 0
        terms, gram = expand_step(e_ref, s_ref, h_ref)

        @pl.when(first)
        def _():
            for w in range(width):
                x_ref[w] = terms[w]()
            g_ref[...] = gram

        @pl.when(jnp.logical_not(first))
        def _():
            for w in range(width):
                x_ref[w] += terms[w]()
            g_ref[...] += gram

    return pl.pallas_call(
        kernel,
        grid_spec=pltpu.PrefetchScalarGridSpec(
            num_scalar_prefetch=1,
            grid=(blocks // step,),
            in_specs=expand_specs(width, step, share, depth, s, k),
            out_specs=[
                pl.BlockSpec((width, s * k, depth), lambda i, sc: (0, 0, 0)),
                pl.BlockSpec((k, 2 * k), lambda i, sc: (0, 0)),
            ],
        ),
        out_shape=[
            jax.ShapeDtypeStruct((width, s * k, depth), f32),
            jax.ShapeDtypeStruct((k, 2 * k), f32),
        ],
        compiler_params=pltpu.CompilerParams(vmem_limit_bytes=20 * MIB),
        cost_estimate=cost(3_300_000_000, 12_000_000),
        name="expand_terms",
    )(core, in_hbm(env), in_hbm(site), half)


def inverse_factor(a, nb):
    n = a.shape[0]
    count = n // 8
    rows = [a[8 * i : 8 * i + 8, :] for i in range(count)]
    lane = lax.broadcasted_iota(jnp.int32, (8, n), 1)
    sub = lax.broadcasted_iota(jnp.int32, (8, n), 0)

    def full(v):
        return jnp.broadcast_to(v, (8, n))

    for j in range(0, n, nb):
        b, o = j // 8, j % 8
        cols = {i: [full(rows[i][:, j + p : j + p + 1]) for p in range(nb)] for i in range(b, count)}
        lines = [full(rows[b][o + q : o + q + 1, :]) for q in range(nb)]
        pivots = [
            [full(cols[b][r][o + q : o + q + 1, :]) for r in range(q + 1)] for q in range(nb)
        ]
        scaled, ratio = [], {}
        for p in range(nb):
            inv = 1.0 / pivots[p][p]
            here = lane == j + p
            line = jnp.where(here, 1.0, lines[p]) * inv
            scaled.append(line)
            for q in range(p + 1, nb):
                ratio[q, p] = pivots[q][p] * inv
            for q in range(p + 1, nb):
                lines[q] = jnp.where(here, 0.0, lines[q]) - pivots[q][p] * line
                for r in range(p + 1, q + 1):
                    pivots[q][r] = pivots[q][r] - pivots[q][p] * ratio[r, p]
        for i in range(b, count):
            c = cols[i]
            value = rows[i]
            for p in range(nb):
                new = jnp.where(lane == j + p, 0.0, value) - c[p] * scaled[p]
                value = jnp.where(sub > o + p, new, value) if i == b else new
                for q in range(p + 1, nb):
                    c[q] = c[q] - c[p] * ratio[q, p]
            rows[i] = value
    w = jnp.concatenate(rows, axis=0)
    row = lax.broadcasted_iota(jnp.int32, (n, n), 0)
    col = lax.broadcasted_iota(jnp.int32, (n, n), 1)
    diagonal = jnp.sum(jnp.where(row == col, w, 0.0), axis=1, keepdims=True)
    unit = jnp.where(row > col, w, 0.0) + jnp.where(row == col, 1.0, 0.0)
    return unit * lax.rsqrt(diagonal)


def split(v):
    high = v.astype(bf16)
    return high, (v - high.astype(f32)).astype(bf16)


def finish(scalars, env, site, half, x_site, g_site, x_own, g_own, own, site_local, operator):
    width, blocks, _, share, depth = env.shape
    s, k = half.shape[1:3]
    step = 4
    last = blocks // step - 1
    pad = operator.shape[0] // 2
    out_rows = pad - 4

    def kernel(
        sc_ref, e_ref, s_ref, h_ref, xs_ref, gs_ref, xo_ref, go_ref, own_ref, oth_ref, sl_ref, m_ref,
        b_ref, give_ref, keep_ref, x_ref, g_ref, p_ref,
    ):
        first = pl.program_id(0) == 0
        terms, gram = expand_step(e_ref, s_ref, h_ref)

        @pl.when(first)
        def _():
            for w in range(width):
                x_ref[w] = xo_ref[w] + terms[w]()
            g_ref[...] = go_ref[...] + gram

        @pl.when(jnp.logical_not(first))
        def _():
            for w in range(width):
                x_ref[w] += terms[w]()
            g_ref[...] += gram

        @pl.when(pl.program_id(0) == last)
        def _():
            gs = gs_ref[...]
            ge = g_ref[:, :k]
            gc = g_ref[:, k:]
            row = lax.broadcasted_iota(jnp.int32, (k, k), 0)
            col = lax.broadcasted_iota(jnp.int32, (k, k), 1)
            trace_site = jnp.sum(jnp.where(row == col, gs, 0.0), keepdims=True)
            trace_expand = jnp.sum(jnp.where(row == col, ge, 0.0), keepdims=True)
            mix = mixing * jnp.sqrt((trace_site + shift_tolerance) / (trace_expand + shift_tolerance))
            inverse = inverse_factor(gs + mix * (gc + gc.T) + (mix * mix) * ge, 8)
            high, low = split(inverse)
            both = jnp.concatenate([high, low], axis=1)

            def apply(v):
                vh, vl = split(v)
                return dot(both, jnp.concatenate([vh, vh], axis=0), ((1,), (0,))) + dot(
                    high, vl, ((1,), (0,))
                )

            for w in range(width):
                for i in range(s):
                    part = slice(i * k, (i + 1) * k)
                    value = apply(xs_ref[w, part] + mix * x_ref[w, part])
                    p_ref[:, pl.ds(w * s + i, k, stride=pad), :] = jnp.stack(
                        [value[:, h * k : (h + 1) * k] for h in range(depth // k)], axis=0
                    )
            for i in range(width * s, pad):
                p_ref[:, pl.ds(i, k, stride=pad), :] = jnp.zeros((depth // k, k, k), f32)
            even = sc_ref[0] == 1
            for i in range(s):
                a0 = own_ref[0, i].astype(f32)
                a1 = oth_ref[0, i].astype(f32)
                rows = jnp.concatenate(
                    [jnp.where(even, a0, a1), jnp.where(even, a1, a0)], axis=1
                )
                done = apply(sl_ref[i] + mix * rows)
                b_ref[:, i * k : (i + 1) * k] = done.T.astype(bf16)

            operator_rows = jnp.concatenate([m_ref[...], m_ref[...]], axis=1)

            def group(g, carry):
                lines = pl.ds(pl.multiple_of(g * (8 * pad), 8 * pad), 8 * pad)
                left = jnp.concatenate(
                    [p_ref[h, lines, :] for h in range(depth // k)], axis=1
                ).astype(bf16)
                paired = dot(left, b_ref[...], ((1,), (0,)))
                for q in range(0, 8, 2):
                    block = jnp.concatenate(
                        [
                            jnp.concatenate(
                                [
                                    paired[r * pad : (r + 1) * pad, t * k : (t + 1) * k]
                                    for t in range(s)
                                ],
                                axis=0,
                            )
                            for r in (q, q + 1)
                        ],
                        axis=1,
                    )
                    bh, bl = split(block)
                    done = dot(operator_rows, jnp.concatenate([bh, bl], axis=0), ((1,), (0,)))
                    for r in (0, 1):
                        piece = done[:, r * k : (r + 1) * k]
                        to = pl.ds(q + r, out_rows, stride=8)
                        give_ref[g, to, :] = piece[:out_rows]
                        keep_ref[g, to, :] = piece[pad : pad + out_rows]
                return carry

            lax.fori_loop(0, k // 8, group, 0)

    fixed3 = lambda i, sc: (0, 0, 0)
    fixed2 = lambda i, sc: (0, 0)
    return pl.pallas_call(
        kernel,
        grid_spec=pltpu.PrefetchScalarGridSpec(
            num_scalar_prefetch=1,
            grid=(blocks // step,),
            in_specs=expand_specs(width, step, share, depth, s, k)
            + [
                pl.BlockSpec((width, s * k, depth), fixed3),
                pl.BlockSpec((k, k), fixed2),
                pl.BlockSpec((width, s * k, depth), fixed3),
                pl.BlockSpec((k, 2 * k), fixed2),
                pl.BlockSpec((1, s, k, share), lambda i, sc: (sc[1], 0, 0, 0)),
                pl.BlockSpec((1, s, k, share), lambda i, sc: (sc[1], 0, 0, 0)),
                pl.BlockSpec((s, k, 2 * share), fixed3),
                pl.BlockSpec(operator.shape, fixed2),
            ],
            out_specs=[
                pl.BlockSpec((2 * share, s * k), fixed2),
                pl.BlockSpec((k // 8, 8 * out_rows, k), fixed3),
                pl.BlockSpec((k // 8, 8 * out_rows, k), fixed3),
            ],
            scratch_shapes=[
                pltpu.VMEM((width, s * k, depth), f32),
                pltpu.VMEM((k, 2 * k), f32),
                pltpu.VMEM((depth // k, k * pad, k), f32),
            ],
        ),
        out_shape=[
            jax.ShapeDtypeStruct((2 * share, s * k), bf16),
            jax.ShapeDtypeStruct((k // 8, 8 * out_rows, k), f32),
            jax.ShapeDtypeStruct((k // 8, 8 * out_rows, k), f32),
        ],
        compiler_params=pltpu.CompilerParams(vmem_limit_bytes=36 * MIB),
        cost_estimate=cost(4_000_000_000, 20_000_000),
        name="finish",
    )(scalars, in_hbm(env), in_hbm(site), half, x_site, g_site, x_own, g_own, own, half, site_local, operator)


def summed_over_chips(half):
    return lax.all_to_all(half, CHIPS, 0, 0, tiled=True).astype(f32).sum(axis=0)


def body(
    environment, site_tensor, mpo_tensor, sketch_site, sketch_expand, row_sectors, column_sectors
):
    mpo_index = lax.axis_index(MPO)
    bond_index = lax.axis_index(BOND)
    core = lax.axis_index(CORE)
    chi, width, depth = environment.shape
    local_rows, physical, _ = site_tensor.shape
    columns = column_sectors.shape[1]
    blocks, share = chi // local_rows, local_rows // 2
    env = jnp.transpose(environment, (1, 0, 2)).reshape(width, blocks, 2, share, depth)
    own_core = core.reshape(1).astype(jnp.int32)
    other_core = 1 - own_core

    operator = lax.dynamic_slice_in_dim(mpo_tensor, mpo_index * width, width, 0)
    operator = jnp.transpose(operator.reshape(width, 4, 2, -1, physical, physical), (2, 1, 3, 5, 0, 4))
    operator = operator.reshape(2, -1, physical, width * physical)
    operator = jnp.pad(operator, ((0, 0), (0, 4), (0, 0), (0, 4)))
    operator = jnp.where(core == 0, operator[::-1], operator).reshape(2 * operator.shape[1], -1)

    sketched, site_y = sketch(site_tensor, sketch_expand, sketch_site, 1024)
    site_y, row_sectors, column_sectors = lax.optimization_barrier(
        (site_y, row_sectors, column_sectors)
    )
    mask_rows = sector_mask(row_sectors, column_sectors)
    site_local = site_y * jnp.transpose(mask_rows, (1, 2, 0))
    site_all = lax.all_gather(site_local.astype(bf16), BOND, axis=0)
    applied = jnp.einsum(
        "vwst,ktwa->vska", mpo_tensor, sketched, preferred_element_type=f32
    ).astype(bf16)
    contracted = lax.all_to_all(applied, MPO, split_axis=0, concat_axis=2, tiled=True)
    contracted = contracted.reshape(width, physical * columns, depth)

    send = expand_half(other_core, env, contracted)
    got = lax.ppermute(send, CORE, SWAP)
    keep = expand_half(own_core, env, contracted)
    half = (keep.astype(f32) + got.astype(f32)).astype(bf16)
    x_site, g_site = site_terms(env, site_all)
    arrived = lax.all_to_all(half.reshape(-1, share, columns), CHIPS, 0, 0, tiled=True)
    piece = arrived.astype(f32).sum(axis=0)
    mask_piece = lax.dynamic_slice(
        mask_rows, (core * share, lax.axis_index("mpo_0"), 0), (share, 1, columns)
    )[:, 0]
    piece = (piece * mask_piece).T.astype(bf16)
    own = lax.all_to_all(
        jnp.broadcast_to(piece[None], (blocks * physical, columns, share)), CHIPS, 0, 0, tiled=True
    )
    own, x_site, g_site = lax.optimization_barrier((own, x_site, g_site))
    own = own.reshape(blocks, physical, columns, share)
    other = lax.ppermute(own, CORE, SWAP)

    x_own, g_own = expand_terms(own_core, env, site_all, own)
    scalars = jnp.concatenate([other_core, bond_index.reshape(1).astype(jnp.int32)])
    basis_flat, give, kept = finish(
        scalars, env, site_all, other, x_site, g_site, x_own, g_own, own, site_local, operator
    )
    basis_local = basis_flat.reshape(local_rows, physical, columns)

    both = (kept + lax.ppermute(give, CORE, SWAP)).astype(bf16)
    chips = blocks * physical
    extended = summed_over_chips(both.reshape(chips, -1, columns))
    extended = jnp.swapaxes(extended.reshape(-1, 8, columns), 0, 1)
    return (basis_local, extended)


def solution(mesh):
    torus = Mesh(mesh.devices.reshape(4, 2, 4, 4), ("mpo_0", "mpo_1", "bond_0", "bond_1"))
    placed = (
        P(None, MPO, BOND),
        P(BOND, None, None),
        P(),
        P(),
        P(MPO, None, None),
        P(None, BOND, None),
        P(),
    )
    return jax.shard_map(
        body,
        mesh=torus,
        in_specs=placed,
        out_specs=(P(BOND, None, None), P(BOND, MPO, None)),
        check_vma=False,
    )
```

```python
import jax
import jax.numpy as jnp
from jax import lax
from jax.experimental import pallas as pl
from jax.experimental.pallas import tpu as pltpu
from jax.sharding import Mesh
from jax.sharding import PartitionSpec as P

MPO = ("mpo_0", "mpo_1")
BOND = ("bond_0", "bond_1")
CHIPS = ("bond_0", "bond_1", "mpo_0")
CORE = "mpo_1"
SWAP = [(0, 1), (1, 0)]

mixing = 0.5
shift_tolerance = 1e-06
f32 = jnp.float32
bf16 = jnp.bfloat16
MIB = 1024 * 1024


def sector_mask(row_labels, column_labels):
    match = (row_labels[0][:, :, None] == column_labels[0][None, None, :]) & (
        row_labels[1][:, :, None] == column_labels[1][None, None, :]
    )
    return match.astype(f32)


def dot(a, b, dims):
    return lax.dot_general(a, b, (dims, ((), ())), preferred_element_type=f32)


def in_hbm(value):
    return pltpu.with_memory_space_constraint(value, pltpu.HBM)


def cost(flops, size):
    return pl.CostEstimate(flops=flops, bytes_accessed=size, transcendentals=0)


def sketch(site_tensor, sketch_expand, sketch_site, width):
    rows, s, depth = site_tensor.shape
    k, v, _ = sketch_expand.shape
    columns = sketch_site.shape[1]
    share = 128
    halves, lines = rows // share, share * s
    last = depth // width - 1

    def kernel(s_ref, o_ref, w_ref, y_ref, z_ref, total, site_total):
        step = pl.program_id(0)
        expand = o_ref[...].reshape(k * v, width)
        for h in range(halves):
            block = s_ref[h * share : (h + 1) * share].reshape(lines, width)

            @pl.when(step == 0)
            def _():
                total[h] = dot(expand, block, ((1,), (1,)))
                site_total[h] = dot(block, w_ref[...], ((1,), (0,)))

            @pl.when(step > 0)
            def _():
                total[h] += dot(expand, block, ((1,), (1,)))
                site_total[h] += dot(block, w_ref[...], ((1,), (0,)))

        @pl.when(step == last)
        def _():
            row = lax.broadcasted_iota(jnp.int32, (lines, lines), 0)
            col = lax.broadcasted_iota(jnp.int32, (lines, lines), 1)
            order = jnp.where((row % s) * share + row // s == col, 1.0, 0.0).astype(bf16)
            for h in range(halves):
                to = slice(h * share, (h + 1) * share)
                y = dot(total[h].astype(bf16), order, ((1,), (0,))).astype(bf16)
                for i in range(k):
                    for t in range(s):
                        y_ref[i, t, :, to] = y[i * v : (i + 1) * v, t * share : (t + 1) * share]
                high, low = split(site_total[h].T)
                z = dot(jnp.concatenate([high, low], axis=0), order, ((1,), (0,)))
                z = z[:columns] + z[columns:]
                for t in range(s):
                    z_ref[t, :, to] = z[:, t * share : (t + 1) * share]

    return pl.pallas_call(
        kernel,
        grid=(last + 1,),
        in_specs=[
            pl.BlockSpec((rows, s, width), lambda i: (0, 0, i)),
            pl.BlockSpec((k, v, width), lambda i: (0, 0, i)),
            pl.BlockSpec((width, columns), lambda i: (i, 0)),
        ],
        out_specs=[
            pl.BlockSpec((k, s, v, rows), lambda i: (0, 0, 0, 0)),
            pl.BlockSpec((s, columns, rows), lambda i: (0, 0, 0)),
        ],
        out_shape=[
            jax.ShapeDtypeStruct((k, s, v, rows), bf16),
            jax.ShapeDtypeStruct((s, columns, rows), f32),
        ],
        scratch_shapes=[
            pltpu.VMEM((halves, k * v, lines), f32),
            pltpu.VMEM((halves, lines, columns), f32),
        ],
        compiler_params=pltpu.CompilerParams(vmem_limit_bytes=36 * MIB),
        cost_estimate=cost(7_000_000_000, 15_000_000),
        name="sketch",
    )(in_hbm(site_tensor), in_hbm(sketch_expand), in_hbm(sketch_site))


def expand_half(core, env, contracted):
    width, blocks, _, share, depth = env.shape
    x = contracted.shape[1]
    k = share
    s = x // k
    step = 4
    steps = blocks // step

    def kernel(core_ref, e_ref, c_ref, o_ref, near, sem):
        core = core_ref[0]
        copies = [
            pltpu.make_async_copy(
                e_ref.at[:, pl.ds(i * step, step), core],
                near.at[:, pl.ds(i * step, step)],
                sem.at[i],
            )
            for i in range(steps)
        ]
        for copy in copies:
            copy.start()
        right = jnp.concatenate([c_ref[w] for w in range(width)], axis=1)
        for i in range(steps):
            copies[i].wait()
            n = pl.ds(i * step, step)
            left = jnp.concatenate(
                [near[w, n].reshape(step * share, depth) for w in range(width)], axis=1
            )
            total = dot(left, right, ((1,), (1,)))
            for t in range(s):
                o_ref[n, t] = total[:, t * k : (t + 1) * k].astype(bf16).reshape(step, share, k)

    return pl.pallas_call(
        kernel,
        in_specs=[
            pl.BlockSpec(memory_space=pltpu.SMEM),
            pl.BlockSpec(memory_space=pl.ANY),
            pl.BlockSpec(memory_space=pltpu.VMEM),
        ],
        out_specs=pl.BlockSpec(memory_space=pltpu.VMEM),
        out_shape=jax.ShapeDtypeStruct((blocks, s, share, k), bf16),
        scratch_shapes=[
            pltpu.VMEM((width, blocks, share, depth), bf16),
            pltpu.SemaphoreType.DMA((steps,)),
        ],
        compiler_params=pltpu.CompilerParams(vmem_limit_bytes=16 * MIB),
        cost_estimate=cost(2 * width * blocks * share * depth * x, 9_000_000),
        name="expand_half",
    )(core, in_hbm(env), contracted)


def site_terms(env, site):
    width, blocks, _, share, depth = env.shape
    rows = 2 * share
    s, k = site.shape[1:3]
    step = 2

    def kernel(e_ref, s_ref, x_ref, g_ref):
        first = pl.program_id(0) == 0
        left = jnp.concatenate([s_ref[z].reshape(s * k, rows) for z in range(step)], axis=1)

        def term(w):
            return dot(left, e_ref[w].reshape(step * rows, depth), ((1,), (0,)))

        wide = jnp.concatenate([left[i * k : (i + 1) * k] for i in range(s)], axis=1)
        gram = dot(wide, wide, ((1,), (1,)))

        @pl.when(first)
        def _():
            for w in range(width):
                x_ref[w] = term(w)
            g_ref[...] = gram

        @pl.when(jnp.logical_not(first))
        def _():
            for w in range(width):
                x_ref[w] += term(w)
            g_ref[...] += gram

    return pl.pallas_call(
        kernel,
        grid=(blocks // step,),
        in_specs=[
            pl.BlockSpec((width, step, 2, share, depth), lambda i: (0, i, 0, 0, 0)),
            pl.BlockSpec((step, s, k, rows), lambda i: (i, 0, 0, 0)),
        ],
        out_specs=[
            pl.BlockSpec((width, s * k, depth), lambda i: (0, 0, 0)),
            pl.BlockSpec((k, k), lambda i: (0, 0)),
        ],
        out_shape=[
            jax.ShapeDtypeStruct((width, s * k, depth), f32),
            jax.ShapeDtypeStruct((k, k), f32),
        ],
        compiler_params=pltpu.CompilerParams(vmem_limit_bytes=20 * MIB),
        cost_estimate=cost(6_000_000_000, 17_000_000),
        name="site_terms",
    )(in_hbm(env), in_hbm(site))


def near_scratch(width, blocks, s, k, share, depth, steps):
    return [
        pltpu.VMEM((width, blocks, share, depth), bf16),
        pltpu.VMEM((blocks, s, k, share), bf16),
        pltpu.VMEM((blocks, s, k, share), bf16),
        pltpu.SemaphoreType.DMA((3, steps)),
    ]


def add_expand(core, e_ref, s_ref, h_ref, near, steps, x_ref, g_ref, x_first, g_first):
    e_near, s_near, h_near, sem = near
    width, blocks, share, depth = e_near.shape
    s, k = h_near.shape[1:3]
    step = blocks // steps
    lanes = pl.ds(pl.multiple_of(core * share, share), share)
    copies = []
    for i in range(steps):
        n = pl.ds(i * step, step)
        copies.append(
            (
                pltpu.make_async_copy(h_ref.at[n], h_near.at[n], sem.at[0, i]),
                pltpu.make_async_copy(e_ref.at[:, n, core], e_near.at[:, n], sem.at[1, i]),
                pltpu.make_async_copy(s_ref.at[n, :, :, lanes], s_near.at[n], sem.at[2, i]),
            )
        )
    for some in copies:
        for copy in some:
            copy.start()
    for i in range(steps):
        for copy in copies[i]:
            copy.wait()
        n = pl.ds(i * step, step)
        half = h_near[n]
        site = s_near[n]
        left = jnp.concatenate([half[z].reshape(s * k, share) for z in range(step)], axis=1)
        for w in range(width):
            term = dot(left, e_near[w, n].reshape(step * share, depth), ((1,), (0,)))
            if i > 0:
                x_ref[w] += term
            else:
                x_ref[w] = term if x_first is None else x_first[w] + term
        wide = jnp.concatenate([left[t * k : (t + 1) * k] for t in range(s)], axis=1)
        other = jnp.concatenate([site[z, t] for t in range(s) for z in range(step)], axis=1)
        gram = dot(wide, jnp.concatenate([wide, other], axis=0), ((1,), (1,)))
        if i > 0:
            g_ref[...] += gram
        else:
            g_ref[...] = gram if g_first is None else g_first[...] + gram


def expand_terms(core, env, site, half):
    width, blocks, _, share, depth = env.shape
    s, k = half.shape[1:3]
    steps = 4

    def kernel(core_ref, e_ref, s_ref, h_ref, x_ref, g_ref, *near):
        add_expand(core_ref[0], e_ref, s_ref, h_ref, near, steps, x_ref, g_ref, None, None)

    return pl.pallas_call(
        kernel,
        in_specs=[pl.BlockSpec(memory_space=pltpu.SMEM)] + [pl.BlockSpec(memory_space=pl.ANY)] * 3,
        out_specs=[pl.BlockSpec(memory_space=pltpu.VMEM)] * 2,
        out_shape=[
            jax.ShapeDtypeStruct((width, s * k, depth), f32),
            jax.ShapeDtypeStruct((k, 2 * k), f32),
        ],
        scratch_shapes=near_scratch(width, blocks, s, k, share, depth, steps),
        compiler_params=pltpu.CompilerParams(vmem_limit_bytes=18 * MIB),
        cost_estimate=cost(3_300_000_000, 12_000_000),
        name="expand_terms",
    )(core, in_hbm(env), in_hbm(site), half)


def inverse_factor(a, nb):
    n = a.shape[0]
    count = n // 8
    rows = [a[8 * i : 8 * i + 8, :] for i in range(count)]
    lane = lax.broadcasted_iota(jnp.int32, (8, n), 1)
    sub = lax.broadcasted_iota(jnp.int32, (8, n), 0)

    def full(v):
        return jnp.broadcast_to(v, (8, n))

    for j in range(0, n, nb):
        b, o = j // 8, j % 8
        cols = {i: [full(rows[i][:, j + p : j + p + 1]) for p in range(nb)] for i in range(b, count)}
        lines = [full(rows[b][o + q : o + q + 1, :]) for q in range(nb)]
        pivots = [
            [full(cols[b][r][o + q : o + q + 1, :]) for r in range(q + 1)] for q in range(nb)
        ]
        scaled, ratio = [], {}
        for p in range(nb):
            inv = 1.0 / pivots[p][p]
            here = lane == j + p
            line = jnp.where(here, 1.0, lines[p]) * inv
            scaled.append(line)
            for q in range(p + 1, nb):
                ratio[q, p] = pivots[q][p] * inv
            for q in range(p + 1, nb):
                lines[q] = jnp.where(here, 0.0, lines[q]) - pivots[q][p] * line
                for r in range(p + 1, q + 1):
                    pivots[q][r] = pivots[q][r] - pivots[q][p] * ratio[r, p]
        for i in range(b, count):
            c = cols[i]
            value = rows[i]
            for p in range(nb):
                new = jnp.where(lane == j + p, 0.0, value) - c[p] * scaled[p]
                value = jnp.where(sub > o + p, new, value) if i == b else new
                for q in range(p + 1, nb):
                    c[q] = c[q] - c[p] * ratio[q, p]
            rows[i] = value
    w = jnp.concatenate(rows, axis=0)
    row = lax.broadcasted_iota(jnp.int32, (n, n), 0)
    col = lax.broadcasted_iota(jnp.int32, (n, n), 1)
    diagonal = jnp.sum(jnp.where(row == col, w, 0.0), axis=1, keepdims=True)
    unit = jnp.where(row > col, w, 0.0) + jnp.where(row == col, 1.0, 0.0)
    return unit * lax.rsqrt(diagonal)


def split(v):
    high = v.astype(bf16)
    return high, (v - high.astype(f32)).astype(bf16)


def finish(scalars, env, site, half, x_site, g_site, x_own, g_own, own, site_local, operator):
    width, blocks, _, share, depth = env.shape
    s, k = half.shape[1:3]
    steps = 4
    pad = operator.shape[0] // 2
    out_rows = pad - 4

    def kernel(
        sc_ref, e_ref, s_ref, h_ref, own_ref, xs_ref, gs_ref, xo_ref, go_ref, sl_ref, m_ref,
        b_ref, give_ref, keep_ref, x_ref, g_ref, p_ref, own_near, own_sem, *near,
    ):
        block = sc_ref[1]
        own_copy = pltpu.make_async_copy(own_ref.at[block], own_near, own_sem)
        own_copy.start()
        add_expand(sc_ref[0], e_ref, s_ref, h_ref, near, steps, x_ref, g_ref, xo_ref, go_ref)
        own_copy.wait()
        h_near = near[2]
        gs = gs_ref[...]
        ge = g_ref[:, :k]
        gc = g_ref[:, k:]
        row = lax.broadcasted_iota(jnp.int32, (k, k), 0)
        col = lax.broadcasted_iota(jnp.int32, (k, k), 1)
        trace_site = jnp.sum(jnp.where(row == col, gs, 0.0), keepdims=True)
        trace_expand = jnp.sum(jnp.where(row == col, ge, 0.0), keepdims=True)
        mix = mixing * jnp.sqrt((trace_site + shift_tolerance) / (trace_expand + shift_tolerance))
        inverse = inverse_factor(gs + mix * (gc + gc.T) + (mix * mix) * ge, 8)
        high, low = split(inverse)
        both = jnp.concatenate([high, low], axis=1)

        def apply(v):
            vh, vl = split(v)
            return dot(both, jnp.concatenate([vh, vh], axis=0), ((1,), (0,))) + dot(
                high, vl, ((1,), (0,))
            )

        for w in range(width):
            for i in range(s):
                part = slice(i * k, (i + 1) * k)
                value = apply(xs_ref[w, part] + mix * x_ref[w, part])
                p_ref[:, pl.ds(w * s + i, k, stride=pad), :] = jnp.stack(
                    [value[:, h * k : (h + 1) * k] for h in range(depth // k)], axis=0
                )
        for i in range(width * s, pad):
            p_ref[:, pl.ds(i, k, stride=pad), :] = jnp.zeros((depth // k, k, k), f32)
        even = sc_ref[0] == 1
        for i in range(s):
            a0 = own_near[i].astype(f32)
            a1 = h_near[block, i].astype(f32)
            rows = jnp.concatenate(
                [jnp.where(even, a0, a1), jnp.where(even, a1, a0)], axis=1
            )
            done = apply(sl_ref[i] + mix * rows)
            b_ref[:, i * k : (i + 1) * k] = done.T.astype(bf16)

        operator_rows = jnp.concatenate([m_ref[...], m_ref[...]], axis=1)

        def group(g):
            lines = pl.ds(pl.multiple_of(g * (8 * pad), 8 * pad), 8 * pad)
            left = jnp.concatenate(
                [p_ref[h, lines, :] for h in range(depth // k)], axis=1
            ).astype(bf16)
            paired = dot(left, b_ref[...], ((1,), (0,)))
            for q in range(0, 8, 2):
                block = jnp.concatenate(
                    [
                        jnp.concatenate(
                            [
                                paired[r * pad : (r + 1) * pad, t * k : (t + 1) * k]
                                for t in range(s)
                            ],
                            axis=0,
                        )
                        for r in (q, q + 1)
                    ],
                    axis=1,
                )
                bh, bl = split(block)
                done = dot(operator_rows, jnp.concatenate([bh, bl], axis=0), ((1,), (0,)))
                for r in (0, 1):
                    piece = done[:, r * k : (r + 1) * k]
                    to = pl.ds(q + r, out_rows, stride=8)
                    give_ref[g, to, :] = piece[:out_rows]
                    keep_ref[g, to, :] = piece[pad : pad + out_rows]

        def groups(i, carry):
            for j in range(4):
                group(i * 4 + j)
            return carry

        lax.fori_loop(0, k // 32, groups, 0)

    return pl.pallas_call(
        kernel,
        in_specs=[pl.BlockSpec(memory_space=pltpu.SMEM)]
        + [pl.BlockSpec(memory_space=pl.ANY)] * 4
        + [pl.BlockSpec(memory_space=pltpu.VMEM)] * 6,
        out_specs=[pl.BlockSpec(memory_space=pltpu.VMEM)] * 3,
        out_shape=[
            jax.ShapeDtypeStruct((2 * share, s * k), bf16),
            jax.ShapeDtypeStruct((k // 8, 8 * out_rows, k), f32),
            jax.ShapeDtypeStruct((k // 8, 8 * out_rows, k), f32),
        ],
        scratch_shapes=[
            pltpu.VMEM((width, s * k, depth), f32),
            pltpu.VMEM((k, 2 * k), f32),
            pltpu.VMEM((depth // k, k * pad, k), f32),
            pltpu.VMEM((s, k, share), bf16),
            pltpu.SemaphoreType.DMA,
        ]
        + near_scratch(width, blocks, s, k, share, depth, steps),
        compiler_params=pltpu.CompilerParams(vmem_limit_bytes=26 * MIB),
        cost_estimate=cost(4_000_000_000, 20_000_000),
        name="finish",
    )(
        scalars, in_hbm(env), in_hbm(site), half, own, x_site, g_site, x_own, g_own, site_local,
        operator,
    )


def summed_over_chips(half):
    return lax.all_to_all(half, CHIPS, 0, 0, tiled=True).astype(f32).sum(axis=0)


def body(
    environment, site_tensor, mpo_tensor, sketch_site, sketch_expand, row_sectors, column_sectors
):
    mpo_index = lax.axis_index(MPO)
    bond_index = lax.axis_index(BOND)
    core = lax.axis_index(CORE)
    chi, width, depth = environment.shape
    local_rows, physical, _ = site_tensor.shape
    columns = column_sectors.shape[1]
    blocks, share = chi // local_rows, local_rows // 2
    env = jnp.transpose(environment, (1, 0, 2)).reshape(width, blocks, 2, share, depth)
    own_core = core.reshape(1).astype(jnp.int32)
    other_core = 1 - own_core

    operator = lax.dynamic_slice_in_dim(mpo_tensor, mpo_index * width, width, 0)
    operator = jnp.transpose(operator.reshape(width, 4, 2, -1, physical, physical), (2, 1, 3, 5, 0, 4))
    operator = operator.reshape(2, -1, physical, width * physical)
    operator = jnp.pad(operator, ((0, 0), (0, 4), (0, 0), (0, 4)))
    operator = jnp.where(core == 0, operator[::-1], operator).reshape(2 * operator.shape[1], -1)

    sketched, site_y = sketch(site_tensor, sketch_expand, sketch_site, 1024)
    site_y, row_sectors, column_sectors = lax.optimization_barrier(
        (site_y, row_sectors, column_sectors)
    )
    mask_rows = sector_mask(row_sectors, column_sectors)
    site_local = site_y * jnp.transpose(mask_rows, (1, 2, 0))
    site_all = lax.all_gather(site_local.astype(bf16), BOND, axis=0)
    applied = jnp.einsum(
        "vwst,ktwa->vska", mpo_tensor, sketched, preferred_element_type=f32
    ).astype(bf16)
    contracted = lax.all_to_all(applied, MPO, split_axis=0, concat_axis=2, tiled=True)
    contracted = contracted.reshape(width, physical * columns, depth)

    send = expand_half(other_core, env, contracted)
    got = lax.ppermute(send, CORE, SWAP)
    keep = expand_half(own_core, env, contracted)
    half = (keep.astype(f32) + got.astype(f32)).astype(bf16)
    x_site, g_site = site_terms(env, site_all)
    arrived = lax.all_to_all(half.reshape(-1, share, columns), CHIPS, 0, 0, tiled=True)
    piece = arrived.astype(f32).sum(axis=0)
    mask_piece = lax.dynamic_slice(
        mask_rows, (core * share, lax.axis_index("mpo_0"), 0), (share, 1, columns)
    )[:, 0]
    piece = (piece * mask_piece).T.astype(bf16)
    own = lax.all_to_all(
        jnp.broadcast_to(piece[None], (blocks * physical, columns, share)), CHIPS, 0, 0, tiled=True
    )
    own, x_site, g_site = lax.optimization_barrier((own, x_site, g_site))
    own = own.reshape(blocks, physical, columns, share)
    other = lax.ppermute(own, CORE, SWAP)

    x_own, g_own = expand_terms(own_core, env, site_all, own)
    scalars = jnp.concatenate([other_core, bond_index.reshape(1).astype(jnp.int32)])
    basis_flat, give, kept = finish(
        scalars, env, site_all, other, x_site, g_site, x_own, g_own, own, site_local, operator
    )
    basis_local = basis_flat.reshape(local_rows, physical, columns)

    both = (kept + lax.ppermute(give, CORE, SWAP)).astype(bf16)
    chips = blocks * physical
    extended = summed_over_chips(both.reshape(chips, -1, columns))
    extended = jnp.swapaxes(extended.reshape(-1, 8, columns), 0, 1)
    return (basis_local, extended)


def solution(mesh):
    torus = Mesh(mesh.devices.reshape(4, 2, 4, 4), ("mpo_0", "mpo_1", "bond_0", "bond_1"))
    placed = (
        P(None, MPO, BOND),
        P(BOND, None, None),
        P(),
        P(),
        P(MPO, None, None),
        P(None, BOND, None),
        P(),
    )
    return jax.shard_map(
        body,
        mesh=torus,
        in_specs=placed,
        out_specs=(P(BOND, None, None), P(BOND, MPO, None)),
        check_vma=False,
    )
```

```python
import functools

import jax
import jax.numpy as jnp
from jax import lax
from jax.experimental import pallas as pl
from jax.experimental.pallas import tpu as pltpu
from jax.sharding import Mesh
from jax.sharding import PartitionSpec as P

MPO = ("mpo_0", "mpo_1")
BOND = ("bond_0", "bond_1")
CHIPS = ("bond_0", "bond_1", "mpo_0")
CORE = "mpo_1"
SWAP = [(0, 1), (1, 0)]

mixing = 0.5
shift_tolerance = 1e-06
f32 = jnp.float32
bf16 = jnp.bfloat16
MIB = 1024 * 1024


def sector_mask(row_labels, column_labels):
    match = (row_labels[0][:, :, None] == column_labels[0][None, None, :]) & (
        row_labels[1][:, :, None] == column_labels[1][None, None, :]
    )
    return match.astype(f32)


def dot(a, b, dims):
    return lax.dot_general(a, b, (dims, ((), ())), preferred_element_type=f32)


def in_hbm(value):
    return pltpu.with_memory_space_constraint(value, pltpu.HBM)


def cost(flops, size):
    return pl.CostEstimate(flops=flops, bytes_accessed=size, transcendentals=0)


def sketch(site_tensor, sketch_expand, sketch_site, width):
    rows, s, depth = site_tensor.shape
    k, v, _ = sketch_expand.shape
    columns = sketch_site.shape[1]
    share = 128
    halves, lines = rows // share, share * s
    last = depth // width - 1

    def kernel(s_ref, o_ref, w_ref, y_ref, z_ref, total, site_total):
        step = pl.program_id(0)
        expand = o_ref[...].reshape(k * v, width)
        for h in range(halves):
            block = s_ref[h * share : (h + 1) * share].reshape(lines, width)

            @pl.when(step == 0)
            def _():
                total[h] = dot(expand, block, ((1,), (1,)))
                site_total[h] = dot(block, w_ref[...], ((1,), (0,)))

            @pl.when(step > 0)
            def _():
                total[h] += dot(expand, block, ((1,), (1,)))
                site_total[h] += dot(block, w_ref[...], ((1,), (0,)))

        @pl.when(step == last)
        def _():
            row = lax.broadcasted_iota(jnp.int32, (lines, lines), 0)
            col = lax.broadcasted_iota(jnp.int32, (lines, lines), 1)
            order = jnp.where((row % s) * share + row // s == col, 1.0, 0.0).astype(bf16)
            for h in range(halves):
                to = slice(h * share, (h + 1) * share)
                y = dot(total[h].astype(bf16), order, ((1,), (0,))).astype(bf16)
                for i in range(k):
                    for t in range(s):
                        y_ref[i, t, :, to] = y[i * v : (i + 1) * v, t * share : (t + 1) * share]
                high, low = split(site_total[h].T)
                z = dot(jnp.concatenate([high, low], axis=0), order, ((1,), (0,)))
                z = z[:columns] + z[columns:]
                for t in range(s):
                    z_ref[t, :, to] = z[:, t * share : (t + 1) * share]

    return pl.pallas_call(
        kernel,
        grid=(last + 1,),
        in_specs=[
            pl.BlockSpec((rows, s, width), lambda i: (0, 0, i)),
            pl.BlockSpec((k, v, width), lambda i: (0, 0, i)),
            pl.BlockSpec((width, columns), lambda i: (i, 0)),
        ],
        out_specs=[
            pl.BlockSpec((k, s, v, rows), lambda i: (0, 0, 0, 0)),
            pl.BlockSpec((s, columns, rows), lambda i: (0, 0, 0)),
        ],
        out_shape=[
            jax.ShapeDtypeStruct((k, s, v, rows), bf16),
            jax.ShapeDtypeStruct((s, columns, rows), f32),
        ],
        scratch_shapes=[
            pltpu.VMEM((halves, k * v, lines), f32),
            pltpu.VMEM((halves, lines, columns), f32),
        ],
        compiler_params=pltpu.CompilerParams(vmem_limit_bytes=36 * MIB),
        cost_estimate=cost(7_000_000_000, 15_000_000),
        name="sketch",
    )(in_hbm(site_tensor), in_hbm(sketch_expand), in_hbm(sketch_site))


def expand_half(core, env, contracted):
    width, blocks, _, share, depth = env.shape
    x = contracted.shape[1]
    k = share
    s = x // k
    step = 4
    steps = blocks // step

    def kernel(core_ref, e_ref, c_ref, o_ref, near, sem):
        core = core_ref[0]
        copies = [
            pltpu.make_async_copy(
                e_ref.at[:, pl.ds(i * step, step), core],
                near.at[:, pl.ds(i * step, step)],
                sem.at[i],
            )
            for i in range(steps)
        ]
        for copy in copies:
            copy.start()
        right = jnp.concatenate([c_ref[w] for w in range(width)], axis=1)
        for i in range(steps):
            copies[i].wait()
            n = pl.ds(i * step, step)
            left = jnp.concatenate(
                [near[w, n].reshape(step * share, depth) for w in range(width)], axis=1
            )
            total = dot(left, right, ((1,), (1,)))
            for t in range(s):
                o_ref[n, t] = total[:, t * k : (t + 1) * k].astype(bf16).reshape(step, share, k)

    return pl.pallas_call(
        kernel,
        in_specs=[
            pl.BlockSpec(memory_space=pltpu.SMEM),
            pl.BlockSpec(memory_space=pl.ANY),
            pl.BlockSpec(memory_space=pltpu.VMEM),
        ],
        out_specs=pl.BlockSpec(memory_space=pltpu.VMEM),
        out_shape=jax.ShapeDtypeStruct((blocks, s, share, k), bf16),
        scratch_shapes=[
            pltpu.VMEM((width, blocks, share, depth), bf16),
            pltpu.SemaphoreType.DMA((steps,)),
        ],
        compiler_params=pltpu.CompilerParams(vmem_limit_bytes=16 * MIB),
        cost_estimate=cost(2 * width * blocks * share * depth * x, 9_000_000),
        name="expand_half",
    )(core, in_hbm(env), contracted)


def site_terms(env, site):
    width, blocks, _, share, depth = env.shape
    rows = 2 * share
    s, k = site.shape[1:3]
    step = 2

    def kernel(e_ref, s_ref, x_ref, g_ref):
        first = pl.program_id(0) == 0
        left = jnp.concatenate([s_ref[z].reshape(s * k, rows) for z in range(step)], axis=1)

        def term(w):
            return dot(left, e_ref[w].reshape(step * rows, depth), ((1,), (0,)))

        wide = jnp.concatenate([left[i * k : (i + 1) * k] for i in range(s)], axis=1)
        gram = dot(wide, wide, ((1,), (1,)))

        @pl.when(first)
        def _():
            for w in range(width):
                x_ref[w] = term(w)
            g_ref[...] = gram

        @pl.when(jnp.logical_not(first))
        def _():
            for w in range(width):
                x_ref[w] += term(w)
            g_ref[...] += gram

    return pl.pallas_call(
        kernel,
        grid=(blocks // step,),
        in_specs=[
            pl.BlockSpec((width, step, 2, share, depth), lambda i: (0, i, 0, 0, 0)),
            pl.BlockSpec((step, s, k, rows), lambda i: (i, 0, 0, 0)),
        ],
        out_specs=[
            pl.BlockSpec((width, s * k, depth), lambda i: (0, 0, 0)),
            pl.BlockSpec((k, k), lambda i: (0, 0)),
        ],
        out_shape=[
            jax.ShapeDtypeStruct((width, s * k, depth), f32),
            jax.ShapeDtypeStruct((k, k), f32),
        ],
        compiler_params=pltpu.CompilerParams(vmem_limit_bytes=20 * MIB),
        cost_estimate=cost(6_000_000_000, 17_000_000),
        name="site_terms",
    )(in_hbm(env), in_hbm(site))


def near_scratch(width, blocks, s, k, share, depth, steps):
    return [
        pltpu.VMEM((width, blocks, share, depth), bf16),
        pltpu.VMEM((blocks, s, k, share), bf16),
        pltpu.VMEM((blocks, s, k, share), bf16),
        pltpu.SemaphoreType.DMA((3, steps)),
    ]


def add_expand(core, e_ref, s_ref, h_ref, near, steps, x_ref, g_ref):
    e_near, s_near, h_near, sem = near
    width, blocks, share, depth = e_near.shape
    s, k = h_near.shape[1:3]
    step = blocks // steps
    lanes = pl.ds(pl.multiple_of(core * share, share), share)
    copies = []
    for i in range(steps):
        n = pl.ds(i * step, step)
        copies.append(
            (
                pltpu.make_async_copy(h_ref.at[n], h_near.at[n], sem.at[0, i]),
                pltpu.make_async_copy(e_ref.at[:, n, core], e_near.at[:, n], sem.at[1, i]),
                pltpu.make_async_copy(s_ref.at[n, :, :, lanes], s_near.at[n], sem.at[2, i]),
            )
        )
    for some in copies:
        for copy in some:
            copy.start()
    for i in range(steps):
        for copy in copies[i]:
            copy.wait()
        n = pl.ds(i * step, step)
        half = h_near[n]
        site = s_near[n]
        left = jnp.concatenate([half[z].reshape(s * k, share) for z in range(step)], axis=1)
        for w in range(width):
            term = dot(left, e_near[w, n].reshape(step * share, depth), ((1,), (0,)))
            if i > 0:
                x_ref[w] += term
            else:
                x_ref[w] = term
        wide = jnp.concatenate([left[t * k : (t + 1) * k] for t in range(s)], axis=1)
        other = jnp.concatenate([site[z, t] for t in range(s) for z in range(step)], axis=1)
        gram = dot(wide, jnp.concatenate([wide, other], axis=0), ((1,), (1,)))
        if i > 0:
            g_ref[...] += gram
        else:
            g_ref[...] = gram


def expand_terms(core, env, site, half):
    width, blocks, _, share, depth = env.shape
    s, k = half.shape[1:3]
    steps = 4

    def kernel(core_ref, e_ref, s_ref, h_ref, x_ref, g_ref, *near):
        add_expand(core_ref[0], e_ref, s_ref, h_ref, near, steps, x_ref, g_ref)

    return pl.pallas_call(
        kernel,
        in_specs=[pl.BlockSpec(memory_space=pltpu.SMEM)] + [pl.BlockSpec(memory_space=pl.ANY)] * 3,
        out_specs=[pl.BlockSpec(memory_space=pltpu.VMEM)] * 2,
        out_shape=[
            jax.ShapeDtypeStruct((width, s * k, depth), f32),
            jax.ShapeDtypeStruct((k, 2 * k), f32),
        ],
        scratch_shapes=near_scratch(width, blocks, s, k, share, depth, steps),
        compiler_params=pltpu.CompilerParams(vmem_limit_bytes=18 * MIB),
        cost_estimate=cost(3_300_000_000, 12_000_000),
        name="expand_terms",
    )(core, in_hbm(env), in_hbm(site), half)


def inverse_factor(a, nb, beside):
    n = a.shape[0]
    count = n // 8
    rows = [a[8 * i : 8 * i + 8, :] for i in range(count)]
    lane = lax.broadcasted_iota(jnp.int32, (8, n), 1)
    sub = lax.broadcasted_iota(jnp.int32, (8, n), 0)

    def full(v):
        return jnp.broadcast_to(v, (8, n))

    for j in range(0, n, nb):
        b, o = j // 8, j % 8
        cols = {i: [full(rows[i][:, j + p : j + p + 1]) for p in range(nb)] for i in range(b, count)}
        lines = [full(rows[b][o + q : o + q + 1, :]) for q in range(nb)]
        pivots = [
            [full(cols[b][r][o + q : o + q + 1, :]) for r in range(q + 1)] for q in range(nb)
        ]
        scaled, ratio = [], {}
        for p in range(nb):
            inv = 1.0 / pivots[p][p]
            here = lane == j + p
            line = jnp.where(here, 1.0, lines[p]) * inv
            scaled.append(line)
            for q in range(p + 1, nb):
                ratio[q, p] = pivots[q][p] * inv
            for q in range(p + 1, nb):
                lines[q] = jnp.where(here, 0.0, lines[q]) - pivots[q][p] * line
                for r in range(p + 1, q + 1):
                    pivots[q][r] = pivots[q][r] - pivots[q][p] * ratio[r, p]
        for i in range(b, count):
            c = cols[i]
            value = rows[i]
            for p in range(nb):
                new = jnp.where(lane == j + p, 0.0, value) - c[p] * scaled[p]
                value = jnp.where(sub > o + p, new, value) if i == b else new
                for q in range(p + 1, nb):
                    c[q] = c[q] - c[p] * ratio[q, p]
            rows[i] = value
        for work in beside[j // nb :: n // nb]:
            work()
    w = jnp.concatenate(rows, axis=0)
    row = lax.broadcasted_iota(jnp.int32, (n, n), 0)
    col = lax.broadcasted_iota(jnp.int32, (n, n), 1)
    diagonal = jnp.sum(jnp.where(row == col, w, 0.0), axis=1, keepdims=True)
    unit = jnp.where(row > col, w, 0.0) + jnp.where(row == col, 1.0, 0.0)
    return unit * lax.rsqrt(diagonal)


def split(v):
    high = v.astype(bf16)
    return high, (v - high.astype(f32)).astype(bf16)


def finish(scalars, env, site, half, x_site, g_site, x_own, g_own, own, site_local, operator):
    width, blocks, _, share, depth = env.shape
    s, k = half.shape[1:3]
    pad = operator.shape[0] // 2
    out_rows = pad - 4

    def kernel(
        sc_ref, e_ref, s_ref, h_ref, own_ref, xs_ref, gs_ref, xo_ref, go_ref, sl_ref, m_ref,
        b_ref, give_ref, keep_ref, x_ref, g_ref, p_ref, stage_ref, own_near, own_sem, *near,
    ):
        block = sc_ref[1]
        own_copy = pltpu.make_async_copy(own_ref.at[block], own_near, own_sem)
        own_copy.start()
        e_near, s_near, h_near, sem = near
        lanes = pl.ds(pl.multiple_of(sc_ref[0] * share, share), share)
        h_copy = pltpu.make_async_copy(h_ref, h_near, sem.at[0, 0])
        s_copy = pltpu.make_async_copy(s_ref.at[:, :, :, lanes], s_near, sem.at[1, 0])
        e_copy = pltpu.make_async_copy(e_ref.at[:, :, sc_ref[0]], e_near, sem.at[2, 0])
        for copy in (h_copy, s_copy, e_copy):
            copy.start()
        h_copy.wait()
        s_copy.wait()
        gram = go_ref[...]
        for t in range(s):
            left = jnp.concatenate([h_near[z, t] for z in range(blocks)], axis=1)
            right = jnp.concatenate([s_near[z, t] for z in range(blocks)], axis=1)
            gram += dot(left, jnp.concatenate([left, right], axis=0), ((1,), (1,)))
        g_ref[...] = gram
        own_copy.wait()
        e_copy.wait()

        def project(w, t):
            left = jnp.concatenate([h_near[z, t] for z in range(blocks)], axis=1)
            part = slice(t * k, (t + 1) * k)
            term = dot(left, e_near[w].reshape(blocks * share, depth), ((1,), (0,)))
            x_ref[w, part] = xo_ref[w, part] + term

        beside = [functools.partial(project, w, t) for w in range(width) for t in range(s)]
        gs = gs_ref[...]
        ge = g_ref[:, :k]
        gc = g_ref[:, k:]
        row = lax.broadcasted_iota(jnp.int32, (k, k), 0)
        col = lax.broadcasted_iota(jnp.int32, (k, k), 1)
        trace_site = jnp.sum(jnp.where(row == col, gs, 0.0), keepdims=True)
        trace_expand = jnp.sum(jnp.where(row == col, ge, 0.0), keepdims=True)
        mix = mixing * jnp.sqrt((trace_site + shift_tolerance) / (trace_expand + shift_tolerance))
        inverse = inverse_factor(gs + mix * (gc + gc.T) + (mix * mix) * ge, 8, beside)
        high, low = split(inverse)
        both = jnp.concatenate([high, low], axis=1)

        def apply(v):
            vh, vl = split(v)
            return dot(both, jnp.concatenate([vh, vh], axis=0), ((1,), (0,))) + dot(
                high, vl, ((1,), (0,))
            )

        for w in range(width):
            for i in range(s):
                part = slice(i * k, (i + 1) * k)
                value = apply(xs_ref[w, part] + mix * x_ref[w, part])
                p_ref[:, pl.ds(w * s + i, k, stride=pad), :] = jnp.stack(
                    [value[:, h * k : (h + 1) * k] for h in range(depth // k)], axis=0
                )
        for i in range(width * s, pad):
            p_ref[:, pl.ds(i, k, stride=pad), :] = jnp.zeros((depth // k, k, k), f32)
        even = sc_ref[0] == 1
        for i in range(s):
            a0 = own_near[i].astype(f32)
            a1 = h_near[block, i].astype(f32)
            rows = jnp.concatenate(
                [jnp.where(even, a0, a1), jnp.where(even, a1, a0)], axis=1
            )
            done = apply(sl_ref[i] + mix * rows)
            b_ref[:, i * k : (i + 1) * k] = done.T.astype(bf16)

        operator_rows = jnp.concatenate([m_ref[...], m_ref[...]], axis=1)

        def group(g, stage):
            lines = pl.ds(pl.multiple_of(g * (8 * pad), 8 * pad), 8 * pad)
            left = jnp.concatenate(
                [p_ref[h, lines, :] for h in range(depth // k)], axis=1
            ).astype(bf16)
            paired = dot(left, b_ref[...], ((1,), (0,)))
            for q in range(0, 8, 2):
                block = jnp.concatenate(
                    [
                        jnp.concatenate(
                            [
                                paired[r * pad : (r + 1) * pad, t * k : (t + 1) * k]
                                for t in range(s)
                            ],
                            axis=0,
                        )
                        for r in (q, q + 1)
                    ],
                    axis=1,
                )
                bh, bl = split(block)
                done = dot(operator_rows, jnp.concatenate([bh, bl], axis=0), ((1,), (0,)))
                for r in (0, 1):
                    piece = done[:, r * k : (r + 1) * k]
                    to = pl.ds(q + r, out_rows, stride=8)
                    stage[to, :] = piece[:out_rows]
                    keep_ref[g, to, :] = piece[pad : pad + out_rows]
            give_ref[g] = stage[...].astype(bf16)

        def groups(i, carry):
            for j in range(4):
                group(i * 4 + j, stage_ref.at[j])
            return carry

        lax.fori_loop(0, k // 32, groups, 0)

    return pl.pallas_call(
        kernel,
        in_specs=[pl.BlockSpec(memory_space=pltpu.SMEM)]
        + [pl.BlockSpec(memory_space=pl.ANY)] * 4
        + [pl.BlockSpec(memory_space=pltpu.VMEM)] * 6,
        out_specs=[pl.BlockSpec(memory_space=pltpu.VMEM)] * 3,
        out_shape=[
            jax.ShapeDtypeStruct((2 * share, s * k), bf16),
            jax.ShapeDtypeStruct((k // 8, 8 * out_rows, k), bf16),
            jax.ShapeDtypeStruct((k // 8, 8 * out_rows, k), f32),
        ],
        scratch_shapes=[
            pltpu.VMEM((width, s * k, depth), f32),
            pltpu.VMEM((k, 2 * k), f32),
            pltpu.VMEM((depth // k, k * pad, k), f32),
            pltpu.VMEM((4, 8 * out_rows, k), f32),
            pltpu.VMEM((s, k, share), bf16),
            pltpu.SemaphoreType.DMA,
        ]
        + near_scratch(width, blocks, s, k, share, depth, 1),
        compiler_params=pltpu.CompilerParams(vmem_limit_bytes=26 * MIB),
        cost_estimate=cost(4_000_000_000, 20_000_000),
        name="finish",
    )(
        scalars, in_hbm(env), in_hbm(site), half, own, x_site, g_site, x_own, g_own, site_local,
        operator,
    )


def summed_over_chips(half):
    return lax.all_to_all(half, CHIPS, 0, 0, tiled=True).astype(f32).sum(axis=0)


def body(
    environment, site_tensor, mpo_tensor, sketch_site, sketch_expand, row_sectors, column_sectors
):
    mpo_index = lax.axis_index(MPO)
    bond_index = lax.axis_index(BOND)
    core = lax.axis_index(CORE)
    chi, width, depth = environment.shape
    local_rows, physical, _ = site_tensor.shape
    columns = column_sectors.shape[1]
    blocks, share = chi // local_rows, local_rows // 2
    env = jnp.transpose(environment, (1, 0, 2)).reshape(width, blocks, 2, share, depth)
    own_core = core.reshape(1).astype(jnp.int32)
    other_core = 1 - own_core

    operator = lax.dynamic_slice_in_dim(mpo_tensor, mpo_index * width, width, 0)
    operator = jnp.transpose(operator.reshape(width, 4, 2, -1, physical, physical), (2, 1, 3, 5, 0, 4))
    operator = operator.reshape(2, -1, physical, width * physical)
    operator = jnp.pad(operator, ((0, 0), (0, 4), (0, 0), (0, 4)))
    operator = jnp.where(core == 0, operator[::-1], operator).reshape(2 * operator.shape[1], -1)

    sketched, site_y = sketch(site_tensor, sketch_expand, sketch_site, 1024)
    site_y, row_sectors, column_sectors = lax.optimization_barrier(
        (site_y, row_sectors, column_sectors)
    )
    mask_rows = sector_mask(row_sectors, column_sectors)
    site_local = site_y * jnp.transpose(mask_rows, (1, 2, 0))
    site_all = lax.all_gather(site_local.astype(bf16), BOND, axis=0)
    applied = jnp.einsum(
        "vwst,ktwa->vska", mpo_tensor, sketched, preferred_element_type=f32
    ).astype(bf16)
    contracted = lax.all_to_all(applied, MPO, split_axis=0, concat_axis=2, tiled=True)
    contracted = contracted.reshape(width, physical * columns, depth)

    send = expand_half(other_core, env, contracted)
    got = lax.ppermute(send, CORE, SWAP)
    keep = expand_half(own_core, env, contracted)
    half = (keep.astype(f32) + got.astype(f32)).astype(bf16)
    x_site, g_site = site_terms(env, site_all)
    arrived = lax.all_to_all(half.reshape(-1, share, columns), CHIPS, 0, 0, tiled=True)
    piece = arrived.astype(f32).sum(axis=0)
    mask_piece = lax.dynamic_slice(
        mask_rows, (core * share, lax.axis_index("mpo_0"), 0), (share, 1, columns)
    )[:, 0]
    piece = (piece * mask_piece).T.astype(bf16)
    own = lax.all_to_all(
        jnp.broadcast_to(piece[None], (blocks * physical, columns, share)), CHIPS, 0, 0, tiled=True
    )
    own, x_site, g_site = lax.optimization_barrier((own, x_site, g_site))
    own = own.reshape(blocks, physical, columns, share)
    other = lax.ppermute(own, CORE, SWAP)

    x_own, g_own = expand_terms(own_core, env, site_all, own)
    scalars = jnp.concatenate([other_core, bond_index.reshape(1).astype(jnp.int32)])
    basis_flat, give, kept = finish(
        scalars, env, site_all, other, x_site, g_site, x_own, g_own, own, site_local, operator
    )
    basis_local = basis_flat.reshape(local_rows, physical, columns)

    both = (kept + lax.ppermute(give, CORE, SWAP).astype(f32)).astype(bf16)
    chips = blocks * physical
    extended = summed_over_chips(both.reshape(chips, -1, columns))
    extended = jnp.swapaxes(extended.reshape(-1, 8, columns), 0, 1)
    return (basis_local, extended)


def solution(mesh):
    torus = Mesh(mesh.devices.reshape(4, 2, 4, 4), ("mpo_0", "mpo_1", "bond_0", "bond_1"))
    placed = (
        P(None, MPO, BOND),
        P(BOND, None, None),
        P(),
        P(),
        P(MPO, None, None),
        P(None, BOND, None),
        P(),
    )
    return jax.shard_map(
        body,
        mesh=torus,
        in_specs=placed,
        out_specs=(P(BOND, None, None), P(BOND, MPO, None)),
        check_vma=False,
    )
```

```python
import functools

import jax
import jax.numpy as jnp
from jax import lax
from jax.experimental import pallas as pl
from jax.experimental.pallas import tpu as pltpu
from jax.sharding import Mesh
from jax.sharding import PartitionSpec as P

MPO = ("mpo_0", "mpo_1")
BOND = ("bond_0", "bond_1")
CHIPS = ("bond_0", "bond_1", "mpo_0")
CORE = "mpo_1"
SWAP = [(0, 1), (1, 0)]

mixing = 0.5
shift_tolerance = 1e-06
f32 = jnp.float32
bf16 = jnp.bfloat16
MIB = 1024 * 1024


def sector_mask(row_labels, column_labels):
    match = (row_labels[0][:, :, None] == column_labels[0][None, None, :]) & (
        row_labels[1][:, :, None] == column_labels[1][None, None, :]
    )
    return match.astype(f32)


def dot(a, b, dims):
    return lax.dot_general(a, b, (dims, ((), ())), preferred_element_type=f32)


def in_hbm(value):
    return pltpu.with_memory_space_constraint(value, pltpu.HBM)


def cost(flops, size):
    return pl.CostEstimate(flops=flops, bytes_accessed=size, transcendentals=0)


def sketch(site_tensor, sketch_expand, sketch_site, width):
    rows, s, depth = site_tensor.shape
    k, v, _ = sketch_expand.shape
    columns = sketch_site.shape[1]
    share = 128
    halves, lines = rows // share, share * s
    last = depth // width - 1

    def kernel(s_ref, o_ref, w_ref, y_ref, z_ref, total, site_total):
        step = pl.program_id(0)
        expand = o_ref[...].reshape(k * v, width)
        for h in range(halves):
            block = s_ref[h * share : (h + 1) * share].reshape(lines, width)

            @pl.when(step == 0)
            def _():
                total[h] = dot(expand, block, ((1,), (1,)))
                site_total[h] = dot(block, w_ref[...], ((1,), (0,)))

            @pl.when(step > 0)
            def _():
                total[h] += dot(expand, block, ((1,), (1,)))
                site_total[h] += dot(block, w_ref[...], ((1,), (0,)))

        @pl.when(step == last)
        def _():
            row = lax.broadcasted_iota(jnp.int32, (lines, lines), 0)
            col = lax.broadcasted_iota(jnp.int32, (lines, lines), 1)
            order = jnp.where((row % s) * share + row // s == col, 1.0, 0.0).astype(bf16)
            for h in range(halves):
                to = slice(h * share, (h + 1) * share)
                y = dot(total[h].astype(bf16), order, ((1,), (0,))).astype(bf16)
                for i in range(k):
                    for t in range(s):
                        y_ref[i, t, :, to] = y[i * v : (i + 1) * v, t * share : (t + 1) * share]
                high, low = split(site_total[h].T)
                z = dot(jnp.concatenate([high, low], axis=0), order, ((1,), (0,)))
                z = z[:columns] + z[columns:]
                for t in range(s):
                    z_ref[t, :, to] = z[:, t * share : (t + 1) * share]

    return pl.pallas_call(
        kernel,
        grid=(last + 1,),
        in_specs=[
            pl.BlockSpec((rows, s, width), lambda i: (0, 0, i)),
            pl.BlockSpec((k, v, width), lambda i: (0, 0, i)),
            pl.BlockSpec((width, columns), lambda i: (i, 0)),
        ],
        out_specs=[
            pl.BlockSpec((k, s, v, rows), lambda i: (0, 0, 0, 0)),
            pl.BlockSpec((s, columns, rows), lambda i: (0, 0, 0)),
        ],
        out_shape=[
            jax.ShapeDtypeStruct((k, s, v, rows), bf16),
            jax.ShapeDtypeStruct((s, columns, rows), f32),
        ],
        scratch_shapes=[
            pltpu.VMEM((halves, k * v, lines), f32),
            pltpu.VMEM((halves, lines, columns), f32),
        ],
        compiler_params=pltpu.CompilerParams(vmem_limit_bytes=36 * MIB),
        cost_estimate=cost(7_000_000_000, 15_000_000),
        name="sketch",
    )(in_hbm(site_tensor), in_hbm(sketch_expand), in_hbm(sketch_site))


def expand_half(core, env, contracted):
    width, blocks, _, share, depth = env.shape
    x = contracted.shape[1]
    k = share
    s = x // k
    step = 4
    steps = blocks // step

    def kernel(core_ref, e_ref, c_ref, o_ref, near, sem):
        core = core_ref[0]
        copies = [
            pltpu.make_async_copy(
                e_ref.at[:, pl.ds(i * step, step), core],
                near.at[:, pl.ds(i * step, step)],
                sem.at[i],
            )
            for i in range(steps)
        ]
        for copy in copies:
            copy.start()
        right = jnp.concatenate([c_ref[w] for w in range(width)], axis=1)
        for i in range(steps):
            copies[i].wait()
            n = pl.ds(i * step, step)
            left = jnp.concatenate(
                [near[w, n].reshape(step * share, depth) for w in range(width)], axis=1
            )
            total = dot(left, right, ((1,), (1,)))
            for t in range(s):
                o_ref[n, t] = total[:, t * k : (t + 1) * k].astype(bf16).reshape(step, share, k)

    return pl.pallas_call(
        kernel,
        in_specs=[
            pl.BlockSpec(memory_space=pltpu.SMEM),
            pl.BlockSpec(memory_space=pl.ANY),
            pl.BlockSpec(memory_space=pltpu.VMEM),
        ],
        out_specs=pl.BlockSpec(memory_space=pltpu.VMEM),
        out_shape=jax.ShapeDtypeStruct((blocks, s, share, k), bf16),
        scratch_shapes=[
            pltpu.VMEM((width, blocks, share, depth), bf16),
            pltpu.SemaphoreType.DMA((steps,)),
        ],
        compiler_params=pltpu.CompilerParams(vmem_limit_bytes=16 * MIB),
        cost_estimate=cost(2 * width * blocks * share * depth * x, 9_000_000),
        name="expand_half",
    )(core, in_hbm(env), contracted)


def site_terms(env, site):
    width, blocks, _, share, depth = env.shape
    rows = 2 * share
    s, k = site.shape[1:3]
    step = 2

    def kernel(e_ref, s_ref, x_ref, g_ref):
        first = pl.program_id(0) == 0
        left = jnp.concatenate([s_ref[z].reshape(s * k, rows) for z in range(step)], axis=1)

        def term(w):
            return dot(left, e_ref[w].reshape(step * rows, depth), ((1,), (0,)))

        wide = jnp.concatenate([left[i * k : (i + 1) * k] for i in range(s)], axis=1)
        gram = dot(wide, wide, ((1,), (1,)))

        @pl.when(first)
        def _():
            for w in range(width):
                x_ref[w] = term(w)
            g_ref[...] = gram

        @pl.when(jnp.logical_not(first))
        def _():
            for w in range(width):
                x_ref[w] += term(w)
            g_ref[...] += gram

    return pl.pallas_call(
        kernel,
        grid=(blocks // step,),
        in_specs=[
            pl.BlockSpec((width, step, 2, share, depth), lambda i: (0, i, 0, 0, 0)),
            pl.BlockSpec((step, s, k, rows), lambda i: (i, 0, 0, 0)),
        ],
        out_specs=[
            pl.BlockSpec((width, s * k, depth), lambda i: (0, 0, 0)),
            pl.BlockSpec((k, k), lambda i: (0, 0)),
        ],
        out_shape=[
            jax.ShapeDtypeStruct((width, s * k, depth), f32),
            jax.ShapeDtypeStruct((k, k), f32),
        ],
        compiler_params=pltpu.CompilerParams(vmem_limit_bytes=20 * MIB),
        cost_estimate=cost(6_000_000_000, 17_000_000),
        name="site_terms",
    )(in_hbm(env), in_hbm(site))


def near_scratch(width, blocks, s, k, share, depth, steps):
    return [
        pltpu.VMEM((width, blocks, share, depth), bf16),
        pltpu.VMEM((blocks, s, k, share), bf16),
        pltpu.VMEM((blocks, s, k, share), bf16),
        pltpu.SemaphoreType.DMA((3, steps)),
    ]


def add_expand(core, e_ref, s_ref, h_ref, near, steps, x_ref, g_ref):
    e_near, s_near, h_near, sem = near
    width, blocks, share, depth = e_near.shape
    s, k = h_near.shape[1:3]
    step = blocks // steps
    lanes = pl.ds(pl.multiple_of(core * share, share), share)
    copies = []
    for i in range(steps):
        n = pl.ds(i * step, step)
        copies.append(
            (
                pltpu.make_async_copy(h_ref.at[n], h_near.at[n], sem.at[0, i]),
                pltpu.make_async_copy(e_ref.at[:, n, core], e_near.at[:, n], sem.at[1, i]),
                pltpu.make_async_copy(s_ref.at[n, :, :, lanes], s_near.at[n], sem.at[2, i]),
            )
        )
    for some in copies:
        for copy in some:
            copy.start()
    for i in range(steps):
        for copy in copies[i]:
            copy.wait()
        n = pl.ds(i * step, step)
        half = h_near[n]
        site = s_near[n]
        left = jnp.concatenate([half[z].reshape(s * k, share) for z in range(step)], axis=1)
        for w in range(width):
            term = dot(left, e_near[w, n].reshape(step * share, depth), ((1,), (0,)))
            if i > 0:
                x_ref[w] += term
            else:
                x_ref[w] = term
        wide = jnp.concatenate([left[t * k : (t + 1) * k] for t in range(s)], axis=1)
        other = jnp.concatenate([site[z, t] for t in range(s) for z in range(step)], axis=1)
        gram = dot(wide, jnp.concatenate([wide, other], axis=0), ((1,), (1,)))
        if i > 0:
            g_ref[...] += gram
        else:
            g_ref[...] = gram


def expand_terms(core, env, site, half):
    width, blocks, _, share, depth = env.shape
    s, k = half.shape[1:3]
    steps = 4

    def kernel(core_ref, e_ref, s_ref, h_ref, x_ref, g_ref, *near):
        add_expand(core_ref[0], e_ref, s_ref, h_ref, near, steps, x_ref, g_ref)

    return pl.pallas_call(
        kernel,
        in_specs=[pl.BlockSpec(memory_space=pltpu.SMEM)] + [pl.BlockSpec(memory_space=pl.ANY)] * 3,
        out_specs=[pl.BlockSpec(memory_space=pltpu.VMEM)] * 2,
        out_shape=[
            jax.ShapeDtypeStruct((width, s * k, depth), f32),
            jax.ShapeDtypeStruct((k, 2 * k), f32),
        ],
        scratch_shapes=near_scratch(width, blocks, s, k, share, depth, steps),
        compiler_params=pltpu.CompilerParams(vmem_limit_bytes=18 * MIB),
        cost_estimate=cost(3_300_000_000, 12_000_000),
        name="expand_terms",
    )(core, in_hbm(env), in_hbm(site), half)


def inverse_factor(a, nb, beside):
    n = a.shape[0]
    count = n // 8
    rows = [a[8 * i : 8 * i + 8, :] for i in range(count)]
    lane = lax.broadcasted_iota(jnp.int32, (8, n), 1)
    sub = lax.broadcasted_iota(jnp.int32, (8, n), 0)

    def full(v):
        return jnp.broadcast_to(v, (8, n))

    for j in range(0, n, nb):
        b, o = j // 8, j % 8
        cols = {i: [full(rows[i][:, j + p : j + p + 1]) for p in range(nb)] for i in range(b, count)}
        lines = [full(rows[b][o + q : o + q + 1, :]) for q in range(nb)]
        pivots = [
            [full(cols[b][r][o + q : o + q + 1, :]) for r in range(q + 1)] for q in range(nb)
        ]
        scaled, ratio = [], {}
        for p in range(nb):
            inv = 1.0 / pivots[p][p]
            here = lane == j + p
            line = jnp.where(here, 1.0, lines[p]) * inv
            scaled.append(line)
            for q in range(p + 1, nb):
                ratio[q, p] = pivots[q][p] * inv
            for q in range(p + 1, nb):
                lines[q] = jnp.where(here, 0.0, lines[q]) - pivots[q][p] * line
                for r in range(p + 1, q + 1):
                    pivots[q][r] = pivots[q][r] - pivots[q][p] * ratio[r, p]
        for i in range(b, count):
            c = cols[i]
            value = rows[i]
            for p in range(nb):
                new = jnp.where(lane == j + p, 0.0, value) - c[p] * scaled[p]
                value = jnp.where(sub > o + p, new, value) if i == b else new
                for q in range(p + 1, nb):
                    c[q] = c[q] - c[p] * ratio[q, p]
            rows[i] = value
        for work in beside[j // nb :: n // nb]:
            work()
    w = jnp.concatenate(rows, axis=0)
    row = lax.broadcasted_iota(jnp.int32, (n, n), 0)
    col = lax.broadcasted_iota(jnp.int32, (n, n), 1)
    diagonal = jnp.sum(jnp.where(row == col, w, 0.0), axis=1, keepdims=True)
    unit = jnp.where(row > col, w, 0.0) + jnp.where(row == col, 1.0, 0.0)
    return unit * lax.rsqrt(diagonal)


def split(v):
    high = v.astype(bf16)
    return high, (v - high.astype(f32)).astype(bf16)


def finish(scalars, env, site, half, x_site, g_site, x_own, g_own, own, site_local, operator):
    width, blocks, _, share, depth = env.shape
    s, k = half.shape[1:3]
    pad = operator.shape[0] // 2
    out_rows = pad - 4

    def kernel(
        sc_ref, e_ref, s_ref, h_ref, own_ref, xs_ref, gs_ref, xo_ref, go_ref, sl_ref, m_ref,
        b_ref, give_ref, keep_ref, x_ref, g_ref, p_ref, stage_ref, own_near, own_sem, *near,
    ):
        block = sc_ref[1]
        own_copy = pltpu.make_async_copy(own_ref.at[block], own_near, own_sem)
        own_copy.start()
        e_near, s_near, h_near, sem = near
        lanes = pl.ds(pl.multiple_of(sc_ref[0] * share, share), share)
        h_copy = pltpu.make_async_copy(h_ref, h_near, sem.at[0, 0])
        s_copy = pltpu.make_async_copy(s_ref.at[:, :, :, lanes], s_near, sem.at[1, 0])
        e_copy = pltpu.make_async_copy(e_ref.at[:, :, sc_ref[0]], e_near, sem.at[2, 0])
        for copy in (h_copy, s_copy, e_copy):
            copy.start()
        h_copy.wait()
        s_copy.wait()
        gram = go_ref[...]
        for t in range(s):
            left = jnp.concatenate([h_near[z, t] for z in range(blocks)], axis=1)
            right = jnp.concatenate([s_near[z, t] for z in range(blocks)], axis=1)
            gram += dot(left, jnp.concatenate([left, right], axis=0), ((1,), (1,)))
        g_ref[...] = gram
        own_copy.wait()
        e_copy.wait()

        def project(w, t):
            left = jnp.concatenate([h_near[z, t] for z in range(blocks)], axis=1)
            part = slice(t * k, (t + 1) * k)
            term = dot(left, e_near[w].reshape(blocks * share, depth), ((1,), (0,)))
            x_ref[w, part] = xo_ref[w, part] + term

        beside = [functools.partial(project, w, t) for w in range(width) for t in range(s)]
        gs = gs_ref[...]
        ge = g_ref[:, :k]
        gc = g_ref[:, k:]
        row = lax.broadcasted_iota(jnp.int32, (k, k), 0)
        col = lax.broadcasted_iota(jnp.int32, (k, k), 1)
        trace_site = jnp.sum(jnp.where(row == col, gs, 0.0), keepdims=True)
        trace_expand = jnp.sum(jnp.where(row == col, ge, 0.0), keepdims=True)
        mix = mixing * jnp.sqrt((trace_site + shift_tolerance) / (trace_expand + shift_tolerance))
        inverse = inverse_factor(gs + mix * (gc + gc.T) + (mix * mix) * ge, 8, beside)
        high, low = split(inverse)
        both = jnp.concatenate([high, low], axis=1)

        def apply(v):
            vh, vl = split(v)
            return dot(both, jnp.concatenate([vh, vh], axis=0), ((1,), (0,))) + dot(
                high, vl, ((1,), (0,))
            )

        for w in range(width):
            for i in range(s):
                part = slice(i * k, (i + 1) * k)
                value = apply(xs_ref[w, part] + mix * x_ref[w, part])
                p_ref[:, pl.ds(w * s + i, k, stride=pad), :] = jnp.stack(
                    [value[:, h * k : (h + 1) * k] for h in range(depth // k)], axis=0
                )
        for i in range(width * s, pad):
            p_ref[:, pl.ds(i, k, stride=pad), :] = jnp.zeros((depth // k, k, k), f32)
        even = sc_ref[0] == 1
        for i in range(s):
            a0 = own_near[i].astype(f32)
            a1 = h_near[block, i].astype(f32)
            rows = jnp.concatenate(
                [jnp.where(even, a0, a1), jnp.where(even, a1, a0)], axis=1
            )
            done = apply(sl_ref[i] + mix * rows)
            b_ref[:, i * k : (i + 1) * k] = done.T.astype(bf16)

        operator_rows = jnp.concatenate([m_ref[...], m_ref[...]], axis=1)

        def group(g, stage):
            lines = pl.ds(pl.multiple_of(g * (8 * pad), 8 * pad), 8 * pad)
            left = jnp.concatenate(
                [p_ref[h, lines, :] for h in range(depth // k)], axis=1
            ).astype(bf16)
            paired = dot(left, b_ref[...], ((1,), (0,)))
            for q in range(0, 8, 2):
                block = jnp.concatenate(
                    [
                        jnp.concatenate(
                            [
                                paired[r * pad : (r + 1) * pad, t * k : (t + 1) * k]
                                for t in range(s)
                            ],
                            axis=0,
                        )
                        for r in (q, q + 1)
                    ],
                    axis=1,
                )
                bh, bl = split(block)
                done = dot(operator_rows, jnp.concatenate([bh, bl], axis=0), ((1,), (0,)))
                for r in (0, 1):
                    piece = done[:, r * k : (r + 1) * k]
                    to = pl.ds(q + r, out_rows, stride=8)
                    stage[to, :] = piece[:out_rows]
                    keep_ref[g, to, :] = piece[pad : pad + out_rows]
            give_ref[g] = stage[...].astype(bf16)

        def groups(i, carry):
            for j in range(4):
                group(i * 4 + j, stage_ref.at[j])
            return carry

        lax.fori_loop(0, k // 32, groups, 0)

    return pl.pallas_call(
        kernel,
        in_specs=[pl.BlockSpec(memory_space=pltpu.SMEM)]
        + [pl.BlockSpec(memory_space=pl.ANY)] * 4
        + [pl.BlockSpec(memory_space=pltpu.VMEM)] * 6,
        out_specs=[pl.BlockSpec(memory_space=pltpu.VMEM)] * 3,
        out_shape=[
            jax.ShapeDtypeStruct((2 * share, s * k), bf16),
            jax.ShapeDtypeStruct((k // 8, 8 * out_rows, k), bf16),
            jax.ShapeDtypeStruct((k // 8, 8 * out_rows, k), f32),
        ],
        scratch_shapes=[
            pltpu.VMEM((width, s * k, depth), f32),
            pltpu.VMEM((k, 2 * k), f32),
            pltpu.VMEM((depth // k, k * pad, k), f32),
            pltpu.VMEM((4, 8 * out_rows, k), f32),
            pltpu.VMEM((s, k, share), bf16),
            pltpu.SemaphoreType.DMA,
        ]
        + near_scratch(width, blocks, s, k, share, depth, 1),
        compiler_params=pltpu.CompilerParams(vmem_limit_bytes=26 * MIB),
        cost_estimate=cost(4_000_000_000, 20_000_000),
        name="finish",
    )(
        scalars, in_hbm(env), in_hbm(site), half, own, x_site, g_site, x_own, g_own, site_local,
        operator,
    )


def summed_over_chips(half):
    return lax.all_to_all(half, CHIPS, 0, 0, tiled=True).astype(f32).sum(axis=0)


def body(
    environment, site_tensor, mpo_tensor, sketch_site, sketch_expand, row_sectors, column_sectors
):
    mpo_index = lax.axis_index(MPO)
    bond_index = lax.axis_index(BOND)
    core = lax.axis_index(CORE)
    chi, width, depth = environment.shape
    local_rows, physical, _ = site_tensor.shape
    columns = column_sectors.shape[1]
    blocks, share = chi // local_rows, local_rows // 2
    env = jnp.transpose(environment, (1, 0, 2)).reshape(width, blocks, 2, share, depth)
    own_core = core.reshape(1).astype(jnp.int32)
    other_core = 1 - own_core

    operator = lax.dynamic_slice_in_dim(mpo_tensor, mpo_index * width, width, 0)
    operator = jnp.transpose(operator.reshape(width, 4, 2, -1, physical, physical), (2, 1, 3, 5, 0, 4))
    operator = operator.reshape(2, -1, physical, width * physical)
    operator = jnp.pad(operator, ((0, 0), (0, 4), (0, 0), (0, 4)))
    operator = jnp.where(core == 0, operator[::-1], operator).reshape(2 * operator.shape[1], -1)

    sketched, site_y = sketch(site_tensor, sketch_expand, sketch_site, 1024)
    site_y, row_sectors, column_sectors = lax.optimization_barrier(
        (site_y, row_sectors, column_sectors)
    )
    mask_rows = sector_mask(row_sectors, column_sectors)
    site_local = site_y * jnp.transpose(mask_rows, (1, 2, 0))
    part = physical // 2
    site_part = lax.dynamic_slice_in_dim(site_local, core * part, part, 0).astype(bf16)
    site_half = lax.all_gather(site_part, BOND, axis=0)
    applied = jnp.einsum(
        "vwst,ktwa->vska", mpo_tensor, sketched, preferred_element_type=f32
    ).astype(bf16)
    contracted = lax.all_to_all(applied, MPO, split_axis=0, concat_axis=2, tiled=True)
    contracted, _ = lax.optimization_barrier((contracted, site_part))
    contracted = contracted.reshape(width, physical * columns, depth)

    send = expand_half(other_core, env, contracted)
    got = lax.ppermute(send, CORE, SWAP)
    keep = expand_half(own_core, env, contracted)
    half = (keep.astype(f32) + got.astype(f32)).astype(bf16)
    arrived = lax.all_to_all(half.reshape(-1, share, columns), CHIPS, 0, 0, tiled=True)
    piece = arrived.astype(f32).sum(axis=0)
    mask_piece = lax.dynamic_slice(
        mask_rows, (core * share, lax.axis_index("mpo_0"), 0), (share, 1, columns)
    )[:, 0]
    piece = (piece * mask_piece).T.astype(bf16)
    site_half, _ = lax.optimization_barrier((site_half, piece))
    site_rest = lax.ppermute(site_half, CORE, SWAP)
    site_all = jnp.where(
        core == 0,
        jnp.concatenate([site_half, site_rest], axis=1),
        jnp.concatenate([site_rest, site_half], axis=1),
    )
    x_site, g_site = site_terms(env, site_all)
    own = lax.all_to_all(
        jnp.broadcast_to(piece[None], (blocks * physical, columns, share)), CHIPS, 0, 0, tiled=True
    )
    own, x_site, g_site = lax.optimization_barrier((own, x_site, g_site))
    own = own.reshape(blocks, physical, columns, share)
    other = lax.ppermute(own, CORE, SWAP)

    x_own, g_own = expand_terms(own_core, env, site_all, own)
    scalars = jnp.concatenate([other_core, bond_index.reshape(1).astype(jnp.int32)])
    basis_flat, give, kept = finish(
        scalars, env, site_all, other, x_site, g_site, x_own, g_own, own, site_local, operator
    )
    basis_local = basis_flat.reshape(local_rows, physical, columns)

    both = (kept + lax.ppermute(give, CORE, SWAP).astype(f32)).astype(bf16)
    chips = blocks * physical
    extended = summed_over_chips(both.reshape(chips, -1, columns))
    extended = jnp.swapaxes(extended.reshape(-1, 8, columns), 0, 1)
    return (basis_local, extended)


def solution(mesh):
    torus = Mesh(mesh.devices.reshape(4, 2, 4, 4), ("mpo_0", "mpo_1", "bond_0", "bond_1"))
    placed = (
        P(None, MPO, BOND),
        P(BOND, None, None),
        P(),
        P(),
        P(MPO, None, None),
        P(None, BOND, None),
        P(),
    )
    return jax.shard_map(
        body,
        mesh=torus,
        in_specs=placed,
        out_specs=(P(BOND, None, None), P(BOND, MPO, None)),
        check_vma=False,
    )
```

```python
import functools

import jax
import jax.numpy as jnp
from jax import lax
from jax.experimental import pallas as pl
from jax.experimental.pallas import tpu as pltpu
from jax.sharding import Mesh
from jax.sharding import PartitionSpec as P

MPO = ("mpo_0", "mpo_1")
BOND = ("bond_0", "bond_1")
CHIPS = ("bond_0", "bond_1", "mpo_0")
CORE = "mpo_1"
SWAP = [(0, 1), (1, 0)]

mixing = 0.5
shift_tolerance = 1e-06
f32 = jnp.float32
bf16 = jnp.bfloat16
MIB = 1024 * 1024


def sector_mask(row_labels, column_labels):
    match = (row_labels[0][:, :, None] == column_labels[0][None, None, :]) & (
        row_labels[1][:, :, None] == column_labels[1][None, None, :]
    )
    return match.astype(f32)


def dot(a, b, dims):
    return lax.dot_general(a, b, (dims, ((), ())), preferred_element_type=f32)


def in_hbm(value):
    return pltpu.with_memory_space_constraint(value, pltpu.HBM)


def cost(flops, size):
    return pl.CostEstimate(flops=flops, bytes_accessed=size, transcendentals=0)


def sketch(site_tensor, sketch_expand, sketch_site, width):
    rows, s, depth = site_tensor.shape
    k, v, _ = sketch_expand.shape
    columns = sketch_site.shape[1]
    share = 128
    halves, lines = rows // share, share * s
    last = depth // width - 1

    def kernel(s_ref, o_ref, w_ref, y_ref, z_ref, total, site_total):
        step = pl.program_id(0)
        expand = o_ref[...].reshape(k * v, width)
        for h in range(halves):
            block = s_ref[h * share : (h + 1) * share].reshape(lines, width)

            @pl.when(step == 0)
            def _():
                total[h] = dot(expand, block, ((1,), (1,)))
                site_total[h] = dot(block, w_ref[...], ((1,), (0,)))

            @pl.when(step > 0)
            def _():
                total[h] += dot(expand, block, ((1,), (1,)))
                site_total[h] += dot(block, w_ref[...], ((1,), (0,)))

        @pl.when(step == last)
        def _():
            row = lax.broadcasted_iota(jnp.int32, (lines, lines), 0)
            col = lax.broadcasted_iota(jnp.int32, (lines, lines), 1)
            order = jnp.where((row % s) * share + row // s == col, 1.0, 0.0).astype(bf16)
            for h in range(halves):
                to = slice(h * share, (h + 1) * share)
                y = dot(total[h].astype(bf16), order, ((1,), (0,))).astype(bf16)
                for i in range(k):
                    for t in range(s):
                        y_ref[i, t, :, to] = y[i * v : (i + 1) * v, t * share : (t + 1) * share]
                high, low = split(site_total[h].T)
                z = dot(jnp.concatenate([high, low], axis=0), order, ((1,), (0,)))
                z = z[:columns] + z[columns:]
                for t in range(s):
                    z_ref[t, :, to] = z[:, t * share : (t + 1) * share]

    return pl.pallas_call(
        kernel,
        grid=(last + 1,),
        in_specs=[
            pl.BlockSpec((rows, s, width), lambda i: (0, 0, i)),
            pl.BlockSpec((k, v, width), lambda i: (0, 0, i)),
            pl.BlockSpec((width, columns), lambda i: (i, 0)),
        ],
        out_specs=[
            pl.BlockSpec((k, s, v, rows), lambda i: (0, 0, 0, 0)),
            pl.BlockSpec((s, columns, rows), lambda i: (0, 0, 0)),
        ],
        out_shape=[
            jax.ShapeDtypeStruct((k, s, v, rows), bf16),
            jax.ShapeDtypeStruct((s, columns, rows), f32),
        ],
        scratch_shapes=[
            pltpu.VMEM((halves, k * v, lines), f32),
            pltpu.VMEM((halves, lines, columns), f32),
        ],
        compiler_params=pltpu.CompilerParams(vmem_limit_bytes=36 * MIB),
        cost_estimate=cost(7_000_000_000, 15_000_000),
        name="sketch",
    )(in_hbm(site_tensor), in_hbm(sketch_expand), in_hbm(sketch_site))


def expand_half(core, env, contracted):
    width, blocks, _, share, depth = env.shape
    x = contracted.shape[1]
    k = share
    s = x // k
    step = 4
    steps = blocks // step

    def kernel(core_ref, e_ref, c_ref, o_ref, near, sem):
        core = core_ref[0]
        copies = [
            pltpu.make_async_copy(
                e_ref.at[:, pl.ds(i * step, step), core],
                near.at[:, pl.ds(i * step, step)],
                sem.at[i],
            )
            for i in range(steps)
        ]
        for copy in copies:
            copy.start()
        right = jnp.concatenate([c_ref[w] for w in range(width)], axis=1)
        for i in range(steps):
            copies[i].wait()
            n = pl.ds(i * step, step)
            left = jnp.concatenate(
                [near[w, n].reshape(step * share, depth) for w in range(width)], axis=1
            )
            total = dot(left, right, ((1,), (1,)))
            for t in range(s):
                o_ref[n, t] = total[:, t * k : (t + 1) * k].astype(bf16).reshape(step, share, k)

    return pl.pallas_call(
        kernel,
        in_specs=[
            pl.BlockSpec(memory_space=pltpu.SMEM),
            pl.BlockSpec(memory_space=pl.ANY),
            pl.BlockSpec(memory_space=pltpu.VMEM),
        ],
        out_specs=pl.BlockSpec(memory_space=pltpu.VMEM),
        out_shape=jax.ShapeDtypeStruct((blocks, s, share, k), bf16),
        scratch_shapes=[
            pltpu.VMEM((width, blocks, share, depth), bf16),
            pltpu.SemaphoreType.DMA((steps,)),
        ],
        compiler_params=pltpu.CompilerParams(vmem_limit_bytes=16 * MIB),
        cost_estimate=cost(2 * width * blocks * share * depth * x, 9_000_000),
        name="expand_half",
    )(core, in_hbm(env), contracted)


def site_terms(env, site):
    width, blocks, _, share, depth = env.shape
    rows = 2 * share
    s, k = site.shape[1:3]
    step = 2

    def kernel(e_ref, s_ref, x_ref, g_ref):
        first = pl.program_id(0) == 0
        left = jnp.concatenate([s_ref[z].reshape(s * k, rows) for z in range(step)], axis=1)

        def term(w):
            return dot(left, e_ref[w].reshape(step * rows, depth), ((1,), (0,)))

        wide = jnp.concatenate([left[i * k : (i + 1) * k] for i in range(s)], axis=1)
        gram = dot(wide, wide, ((1,), (1,)))

        @pl.when(first)
        def _():
            for w in range(width):
                x_ref[w] = term(w)
            g_ref[...] = gram

        @pl.when(jnp.logical_not(first))
        def _():
            for w in range(width):
                x_ref[w] += term(w)
            g_ref[...] += gram

    return pl.pallas_call(
        kernel,
        grid=(blocks // step,),
        in_specs=[
            pl.BlockSpec((width, step, 2, share, depth), lambda i: (0, i, 0, 0, 0)),
            pl.BlockSpec((step, s, k, rows), lambda i: (i, 0, 0, 0)),
        ],
        out_specs=[
            pl.BlockSpec((width, s * k, depth), lambda i: (0, 0, 0)),
            pl.BlockSpec((k, k), lambda i: (0, 0)),
        ],
        out_shape=[
            jax.ShapeDtypeStruct((width, s * k, depth), f32),
            jax.ShapeDtypeStruct((k, k), f32),
        ],
        compiler_params=pltpu.CompilerParams(vmem_limit_bytes=20 * MIB),
        cost_estimate=cost(6_000_000_000, 17_000_000),
        name="site_terms",
    )(in_hbm(env), in_hbm(site))


def near_scratch(width, blocks, s, k, share, depth, steps):
    return [
        pltpu.VMEM((width, blocks, share, depth), bf16),
        pltpu.VMEM((blocks, s, k, share), bf16),
        pltpu.VMEM((blocks, s, k, share), bf16),
        pltpu.SemaphoreType.DMA((3, steps)),
    ]


def add_expand(core, e_ref, s_ref, h_ref, near, steps, x_ref, g_ref):
    e_near, s_near, h_near, sem = near
    width, blocks, share, depth = e_near.shape
    s, k = h_near.shape[1:3]
    step = blocks // steps
    lanes = pl.ds(pl.multiple_of(core * share, share), share)
    copies = []
    for i in range(steps):
        n = pl.ds(i * step, step)
        copies.append(
            (
                pltpu.make_async_copy(h_ref.at[n], h_near.at[n], sem.at[0, i]),
                pltpu.make_async_copy(e_ref.at[:, n, core], e_near.at[:, n], sem.at[1, i]),
                pltpu.make_async_copy(s_ref.at[n, :, :, lanes], s_near.at[n], sem.at[2, i]),
            )
        )
    for some in copies:
        for copy in some:
            copy.start()
    for i in range(steps):
        for copy in copies[i]:
            copy.wait()
        n = pl.ds(i * step, step)
        half = h_near[n]
        site = s_near[n]
        left = jnp.concatenate([half[z].reshape(s * k, share) for z in range(step)], axis=1)
        for w in range(width):
            term = dot(left, e_near[w, n].reshape(step * share, depth), ((1,), (0,)))
            if i > 0:
                x_ref[w] += term
            else:
                x_ref[w] = term
        wide = jnp.concatenate([left[t * k : (t + 1) * k] for t in range(s)], axis=1)
        other = jnp.concatenate([site[z, t] for t in range(s) for z in range(step)], axis=1)
        gram = dot(wide, jnp.concatenate([wide, other], axis=0), ((1,), (1,)))
        if i > 0:
            g_ref[...] += gram
        else:
            g_ref[...] = gram


def expand_terms(core, env, site, half):
    width, blocks, _, share, depth = env.shape
    s, k = half.shape[1:3]
    steps = 4

    def kernel(core_ref, e_ref, s_ref, h_ref, x_ref, g_ref, *near):
        add_expand(core_ref[0], e_ref, s_ref, h_ref, near, steps, x_ref, g_ref)

    return pl.pallas_call(
        kernel,
        in_specs=[pl.BlockSpec(memory_space=pltpu.SMEM)] + [pl.BlockSpec(memory_space=pl.ANY)] * 3,
        out_specs=[pl.BlockSpec(memory_space=pltpu.VMEM)] * 2,
        out_shape=[
            jax.ShapeDtypeStruct((width, s * k, depth), f32),
            jax.ShapeDtypeStruct((k, 2 * k), f32),
        ],
        scratch_shapes=near_scratch(width, blocks, s, k, share, depth, steps),
        compiler_params=pltpu.CompilerParams(vmem_limit_bytes=18 * MIB),
        cost_estimate=cost(3_300_000_000, 12_000_000),
        name="expand_terms",
    )(core, in_hbm(env), in_hbm(site), half)


def inverse_factor(a, nb, beside):
    n = a.shape[0]
    count = n // 8
    rows = [a[8 * i : 8 * i + 8, :] for i in range(count)]
    lane = lax.broadcasted_iota(jnp.int32, (8, n), 1)
    sub = lax.broadcasted_iota(jnp.int32, (8, n), 0)

    def full(v):
        return jnp.broadcast_to(v, (8, n))

    for j in range(0, n, nb):
        b, o = j // 8, j % 8
        cols = {i: [full(rows[i][:, j + p : j + p + 1]) for p in range(nb)] for i in range(b, count)}
        lines = [full(rows[b][o + q : o + q + 1, :]) for q in range(nb)]
        pivots = [
            [full(cols[b][r][o + q : o + q + 1, :]) for r in range(q + 1)] for q in range(nb)
        ]
        scaled, ratio = [], {}
        for p in range(nb):
            inv = 1.0 / pivots[p][p]
            here = lane == j + p
            line = jnp.where(here, 1.0, lines[p]) * inv
            scaled.append(line)
            for q in range(p + 1, nb):
                ratio[q, p] = pivots[q][p] * inv
            for q in range(p + 1, nb):
                lines[q] = jnp.where(here, 0.0, lines[q]) - pivots[q][p] * line
                for r in range(p + 1, q + 1):
                    pivots[q][r] = pivots[q][r] - pivots[q][p] * ratio[r, p]
        for i in range(b, count):
            c = cols[i]
            value = rows[i]
            for p in range(nb):
                new = jnp.where(lane == j + p, 0.0, value) - c[p] * scaled[p]
                value = jnp.where(sub > o + p, new, value) if i == b else new
                for q in range(p + 1, nb):
                    c[q] = c[q] - c[p] * ratio[q, p]
            rows[i] = value
        for work in beside[j // nb :: n // nb]:
            work()
    w = jnp.concatenate(rows, axis=0)
    row = lax.broadcasted_iota(jnp.int32, (n, n), 0)
    col = lax.broadcasted_iota(jnp.int32, (n, n), 1)
    diagonal = jnp.sum(jnp.where(row == col, w, 0.0), axis=1, keepdims=True)
    unit = jnp.where(row > col, w, 0.0) + jnp.where(row == col, 1.0, 0.0)
    return unit * lax.rsqrt(diagonal)


def split(v):
    high = v.astype(bf16)
    return high, (v - high.astype(f32)).astype(bf16)


def finish(scalars, env, site, half, x_site, g_site, x_own, g_own, own, site_local, operator):
    width, blocks, _, share, depth = env.shape
    s, k = half.shape[1:3]
    pad = operator.shape[0] // 2
    out_rows = pad - 4

    def kernel(
        sc_ref, e_ref, s_ref, h_ref, own_ref, xs_ref, gs_ref, xo_ref, go_ref, sl_ref, m_ref,
        b_ref, give_ref, keep_ref, x_ref, g_ref, p_ref, stage_ref, own_near, own_sem, *near,
    ):
        block = sc_ref[1]
        own_copy = pltpu.make_async_copy(own_ref.at[block], own_near, own_sem)
        own_copy.start()
        e_near, s_near, h_near, sem = near
        lanes = pl.ds(pl.multiple_of(sc_ref[0] * share, share), share)
        h_copy = pltpu.make_async_copy(h_ref, h_near, sem.at[0, 0])
        s_copy = pltpu.make_async_copy(s_ref.at[:, :, :, lanes], s_near, sem.at[1, 0])
        e_copy = pltpu.make_async_copy(e_ref.at[:, :, sc_ref[0]], e_near, sem.at[2, 0])
        for copy in (h_copy, s_copy, e_copy):
            copy.start()
        h_copy.wait()
        s_copy.wait()
        gram = go_ref[...]
        for t in range(s):
            left = jnp.concatenate([h_near[z, t] for z in range(blocks)], axis=1)
            right = jnp.concatenate([s_near[z, t] for z in range(blocks)], axis=1)
            gram += dot(left, jnp.concatenate([left, right], axis=0), ((1,), (1,)))
        g_ref[...] = gram
        own_copy.wait()
        e_copy.wait()

        def project(w, t):
            left = jnp.concatenate([h_near[z, t] for z in range(blocks)], axis=1)
            part = slice(t * k, (t + 1) * k)
            term = dot(left, e_near[w].reshape(blocks * share, depth), ((1,), (0,)))
            x_ref[w, part] = xo_ref[w, part] + term

        beside = [functools.partial(project, w, t) for w in range(width) for t in range(s)]
        gs = gs_ref[...]
        ge = g_ref[:, :k]
        gc = g_ref[:, k:]
        row = lax.broadcasted_iota(jnp.int32, (k, k), 0)
        col = lax.broadcasted_iota(jnp.int32, (k, k), 1)
        trace_site = jnp.sum(jnp.where(row == col, gs, 0.0), keepdims=True)
        trace_expand = jnp.sum(jnp.where(row == col, ge, 0.0), keepdims=True)
        mix = mixing * jnp.sqrt((trace_site + shift_tolerance) / (trace_expand + shift_tolerance))
        inverse = inverse_factor(gs + mix * (gc + gc.T) + (mix * mix) * ge, 8, beside)
        high, low = split(inverse)
        both = jnp.concatenate([high, low], axis=1)

        def apply(v):
            vh, vl = split(v)
            return dot(both, jnp.concatenate([vh, vh], axis=0), ((1,), (0,))) + dot(
                high, vl, ((1,), (0,))
            )

        for w in range(width):
            for i in range(s):
                part = slice(i * k, (i + 1) * k)
                value = apply(xs_ref[w, part] + mix * x_ref[w, part])
                p_ref[:, pl.ds(w * s + i, k, stride=pad), :] = jnp.stack(
                    [value[:, h * k : (h + 1) * k] for h in range(depth // k)], axis=0
                )
        for i in range(width * s, pad):
            p_ref[:, pl.ds(i, k, stride=pad), :] = jnp.zeros((depth // k, k, k), f32)
        even = sc_ref[0] == 1
        for i in range(s):
            a0 = own_near[i].astype(f32)
            a1 = h_near[block, i].astype(f32)
            rows = jnp.concatenate(
                [jnp.where(even, a0, a1), jnp.where(even, a1, a0)], axis=1
            )
            done = apply(sl_ref[i] + mix * rows)
            b_ref[:, i * k : (i + 1) * k] = done.T.astype(bf16)

        operator_rows = jnp.concatenate([m_ref[...], m_ref[...]], axis=1)

        def group(g, stage):
            lines = pl.ds(pl.multiple_of(g * (8 * pad), 8 * pad), 8 * pad)
            left = jnp.concatenate(
                [p_ref[h, lines, :] for h in range(depth // k)], axis=1
            ).astype(bf16)
            paired = dot(left, b_ref[...], ((1,), (0,)))
            for q in range(0, 8, 2):
                block = jnp.concatenate(
                    [
                        jnp.concatenate(
                            [
                                paired[r * pad : (r + 1) * pad, t * k : (t + 1) * k]
                                for t in range(s)
                            ],
                            axis=0,
                        )
                        for r in (q, q + 1)
                    ],
                    axis=1,
                )
                bh, bl = split(block)
                done = dot(operator_rows, jnp.concatenate([bh, bl], axis=0), ((1,), (0,)))
                for r in (0, 1):
                    piece = done[:, r * k : (r + 1) * k]
                    to = pl.ds(q + r, out_rows, stride=8)
                    stage[to, :] = piece[:out_rows]
                    keep_ref[g, to, :] = piece[pad : pad + out_rows]
            give_ref[g] = stage[...].astype(bf16)

        def groups(i, carry):
            for j in range(8):
                group(i * 8 + j, stage_ref.at[j])
            return carry

        lax.fori_loop(0, k // 64, groups, 0)

    return pl.pallas_call(
        kernel,
        in_specs=[pl.BlockSpec(memory_space=pltpu.SMEM)]
        + [pl.BlockSpec(memory_space=pl.ANY)] * 4
        + [pl.BlockSpec(memory_space=pltpu.VMEM)] * 6,
        out_specs=[pl.BlockSpec(memory_space=pltpu.VMEM)] * 3,
        out_shape=[
            jax.ShapeDtypeStruct((2 * share, s * k), bf16),
            jax.ShapeDtypeStruct((k // 8, 8 * out_rows, k), bf16),
            jax.ShapeDtypeStruct((k // 8, 8 * out_rows, k), f32),
        ],
        scratch_shapes=[
            pltpu.VMEM((width, s * k, depth), f32),
            pltpu.VMEM((k, 2 * k), f32),
            pltpu.VMEM((depth // k, k * pad, k), f32),
            pltpu.VMEM((8, 8 * out_rows, k), f32),
            pltpu.VMEM((s, k, share), bf16),
            pltpu.SemaphoreType.DMA,
        ]
        + near_scratch(width, blocks, s, k, share, depth, 1),
        compiler_params=pltpu.CompilerParams(vmem_limit_bytes=26 * MIB),
        cost_estimate=cost(4_000_000_000, 20_000_000),
        name="finish",
    )(
        scalars, in_hbm(env), in_hbm(site), half, own, x_site, g_site, x_own, g_own, site_local,
        operator,
    )


def summed_over_chips(half):
    return lax.all_to_all(half, CHIPS, 0, 0, tiled=True).astype(f32).sum(axis=0)


def body(
    environment, site_tensor, mpo_tensor, sketch_site, sketch_expand, row_sectors, column_sectors
):
    mpo_index = lax.axis_index(MPO)
    bond_index = lax.axis_index(BOND)
    core = lax.axis_index(CORE)
    chi, width, depth = environment.shape
    local_rows, physical, _ = site_tensor.shape
    columns = column_sectors.shape[1]
    blocks, share = chi // local_rows, local_rows // 2
    env = jnp.transpose(environment, (1, 0, 2)).reshape(width, blocks, 2, share, depth)
    own_core = core.reshape(1).astype(jnp.int32)
    other_core = 1 - own_core

    operator = lax.dynamic_slice_in_dim(mpo_tensor, mpo_index * width, width, 0)
    operator = jnp.transpose(operator.reshape(width, 4, 2, -1, physical, physical), (2, 1, 3, 5, 0, 4))
    operator = operator.reshape(2, -1, physical, width * physical)
    operator = jnp.pad(operator, ((0, 0), (0, 4), (0, 0), (0, 4)))
    operator = jnp.where(core == 0, operator[::-1], operator).reshape(2 * operator.shape[1], -1)

    sketched, site_y = sketch(site_tensor, sketch_expand, sketch_site, 1024)
    site_y, row_sectors, column_sectors = lax.optimization_barrier(
        (site_y, row_sectors, column_sectors)
    )
    mask_rows = sector_mask(row_sectors, column_sectors)
    site_local = site_y * jnp.transpose(mask_rows, (1, 2, 0))
    site_all = lax.all_gather(site_local.astype(bf16), BOND, axis=0)
    applied = jnp.einsum(
        "vwst,ktwa->vska", mpo_tensor, sketched, preferred_element_type=f32
    ).astype(bf16)
    contracted = lax.all_to_all(applied, MPO, split_axis=0, concat_axis=2, tiled=True)
    contracted = contracted.reshape(width, physical * columns, depth)

    send = expand_half(other_core, env, contracted)
    got = lax.ppermute(send, CORE, SWAP)
    keep = expand_half(own_core, env, contracted)
    half = (keep.astype(f32) + got.astype(f32)).astype(bf16)
    x_site, g_site = site_terms(env, site_all)
    arrived = lax.all_to_all(half.reshape(-1, share, columns), CHIPS, 0, 0, tiled=True)
    piece = arrived.astype(f32).sum(axis=0)
    mask_piece = lax.dynamic_slice(
        mask_rows, (core * share, lax.axis_index("mpo_0"), 0), (share, 1, columns)
    )[:, 0]
    piece = (piece * mask_piece).T.astype(bf16)
    own = lax.all_to_all(
        jnp.broadcast_to(piece[None], (blocks * physical, columns, share)), CHIPS, 0, 0, tiled=True
    )
    own, x_site, g_site = lax.optimization_barrier((own, x_site, g_site))
    own = own.reshape(blocks, physical, columns, share)
    other = lax.ppermute(own, CORE, SWAP)

    x_own, g_own = expand_terms(own_core, env, site_all, own)
    scalars = jnp.concatenate([other_core, bond_index.reshape(1).astype(jnp.int32)])
    basis_flat, give, kept = finish(
        scalars, env, site_all, other, x_site, g_site, x_own, g_own, own, site_local, operator
    )
    basis_local = basis_flat.reshape(local_rows, physical, columns)

    both = (kept + lax.ppermute(give, CORE, SWAP).astype(f32)).astype(bf16)
    chips = blocks * physical
    extended = summed_over_chips(both.reshape(chips, -1, columns))
    extended = jnp.swapaxes(extended.reshape(-1, 8, columns), 0, 1)
    return (basis_local, extended)


def solution(mesh):
    torus = Mesh(mesh.devices.reshape(4, 2, 4, 4), ("mpo_0", "mpo_1", "bond_0", "bond_1"))
    placed = (
        P(None, MPO, BOND),
        P(BOND, None, None),
        P(),
        P(),
        P(MPO, None, None),
        P(None, BOND, None),
        P(),
    )
    return jax.shard_map(
        body,
        mesh=torus,
        in_specs=placed,
        out_specs=(P(BOND, None, None), P(BOND, MPO, None)),
        check_vma=False,
    )
```
